512 devices in a mesh: row: 64 (over x, z, core), col: 8 (over y).
Axes of the slice: x: 4, y: 8, z: 8, core: 2. Of those that a mesh axis runs over, the one named last changes fastest.
Arguments:
- matrix: float32 [16384, 16384], P('row', 'col'), as said below
Outputs:
- reduced: float32 [16384, 16384], P('row', 'col')
Inputs may be any that keep to these rules, and one draw needn't show every extreme that they name: matrix is symmetric.
All inputs are finite; a program needn't handle non-finite values.
Results may differ from the reference program's by a relative error of at most 0.00012.
Values sent between devices are 32-bit elements; how exact they have to be, the bound alone decides.
A program may use at most 64 MiB of HBM per device.

```python
import jax
import jax.numpy as jnp
from jax import lax

N = 16384
B = 96
PANELS = 2


def draw_matrix(key, part):
    key = jax.random.fold_in(key, 11)
    noise_key = jax.random.fold_in(key, 0)
    noise = jax.random.normal(noise_key, (N, N), jnp.float32)
    symmetric = (noise + noise.T) * 0.7071
    return symmetric


def setup_inputs(seed: int = 0) -> dict:
    key_list = jax.random.split(jax.random.key(seed), 2)
    matrix = draw_matrix(jax.random.fold_in(key_list[1], 71), 0)
    return {"matrix": matrix}


HIGH = lax.Precision.HIGHEST

def unit_lower_upper(square):
    size = square.shape[0]
    index = jnp.arange(size)

    def step(k, carry):
        work, multipliers = carry
        pivot_row = lax.dynamic_index_in_dim(work, k, 0, keepdims=False)
        column = lax.dynamic_index_in_dim(work, k, 1, keepdims=False)
        ratio = jnp.where(index > k, column / pivot_row[k], 0.0)
        work = work - ratio[:, None] * pivot_row[None, :]
        multipliers = multipliers + ratio[:, None] * (index[None, :] == k).astype(square.dtype)
        return (work, multipliers)
    work, multipliers = lax.fori_loop(0, size, step, (square, jnp.zeros_like(square)))
    return (multipliers + jnp.eye(size, dtype=square.dtype), jnp.triu(work))

def panel_update(current, start):
    trail = start + B
    rows = jnp.arange(N)
    live = (rows >= trail)[:, None]
    panel = jnp.where(live, current[:, start:start + B], 0.0)
    gram = jnp.dot(panel.T, panel, precision=HIGH)
    top = panel[trail:trail + B]
    chol = jnp.linalg.cholesky(gram)
    ortho = jax.scipy.linalg.solve_triangular(chol, panel.T, lower=True).T
    top_ortho = jax.scipy.linalg.solve_triangular(chol, top.T, lower=True).T
    unit_lower, upper = unit_lower_upper(jnp.eye(B, dtype=current.dtype) - top_ortho)
    unit_rows = (rows[:, None] == trail + jnp.arange(B)[None, :]).astype(current.dtype)
    kernel = jnp.where(live, unit_rows - ortho, 0.0)
    basis = jax.scipy.linalg.solve_triangular(upper.T, kernel.T, lower=True).T
    factor = jax.scipy.linalg.solve_triangular(unit_lower, upper.T, lower=True, unit_diagonal=True).T
    image = jnp.dot(jnp.dot(current, basis, precision=HIGH), factor, precision=HIGH)
    coupling = jnp.dot(factor.T, jnp.dot(basis.T, image, precision=HIGH), precision=HIGH)
    half = image - 0.5 * jnp.dot(basis, coupling, precision=HIGH)
    return current - jnp.dot(half, basis.T, precision=HIGH) - jnp.dot(basis, half.T, precision=HIGH)

def reference(matrix):
    current = matrix
    for panel_index in range(PANELS):
        current = panel_update(current, panel_index * B)
    return current
```

```python
import jax
import jax.numpy as jnp
from jax import lax
from jax.experimental import pallas as pl
from jax.experimental.pallas import tpu as pltpu
from jax.sharding import PartitionSpec as P

B = 96
ROWS = 256
COLS = 2048
NX, NZ, NY = 4, 8, 8
F32 = jnp.float32
HIGH = lax.Precision.HIGHEST
MESH = pl.DeviceIdType.MESH

SEND_SEMS = 320


def nn(a, b):
    return lax.dot_general(a, b, (((1,), (0,)), ((), ())), precision=HIGH, preferred_element_type=F32)


def nt(a, b):
    return lax.dot_general(a, b, (((1,), (1,)), ((), ())), precision=HIGH, preferred_element_type=F32)


class Links:
    def __init__(self, send, recv):
        self.send, self.recv, self.count, self.open = send, recv, 0, []
        row, self.y = lax.axis_index("row"), lax.axis_index("col")
        self.row = row
        self.x, self.z, self.k = row // 16, (row // 2) % 8, row % 2

    def sems(self, n):
        first = self.count
        self.count += n
        return first

    def at(self, kind, j):
        x, z, k, y = self.x, self.z, self.k, self.y
        if kind == "x":
            x = (x + j) % NX
        elif kind == "z":
            z = (z + j) % NZ
        elif kind == "k":
            k = (k + j) % 2
        else:
            y = (y + j) % NY
        return (x * 16 + z * 2 + k, y)

    def copy(self, src, dst, sem, kind, j):
        return pltpu.make_async_remote_copy(
            src_ref=src, dst_ref=dst, send_sem=self.send.at[sem], recv_sem=self.recv.at[sem],
            device_id=self.at(kind, j), device_id_type=MESH)

    def finish(self):
        for copy in self.open:
            copy.wait_send()


SIZE = {"x": NX, "z": NZ, "y": NY, "k": 2}


def exchange(links, kind, src_of, dst_of):
    n = SIZE[kind]
    first = links.sems(n)
    copies = []
    for j in range(1, n):
        copy = links.copy(src_of(j), dst_of(j), first + j, kind, j)
        copy.start()
        copies.append(copy)
    links.open += copies
    return copies


def arrive(copies):
    for copy in copies:
        copy.wait_recv()


def place(links, kind, j):
    return (getattr(links, kind) + j) % SIZE[kind]


def ypiece(j):
    return pl.ds(pl.multiple_of(24 * (j // 2), 8), 24), pl.ds(pl.multiple_of(128 * (j % 2), 128), 128)


def zpiece(j):
    return ypiece_rows(j), pl.ds(pl.multiple_of(128 * (j // 2), 128), 128)


def ypiece_rows(j):
    return pl.ds(pl.multiple_of(24 * (j % 2), 8), 24)


def zregion(links):
    return (pl.ds(pl.multiple_of(48 * links.k + 24 * (links.z % 2), 8), 24),
            pl.ds(pl.multiple_of(512 * links.x + 128 * (links.z // 2), 128), 128))


def xregion(links):
    return (pl.ds(pl.multiple_of(48 * links.k, 8), 48),
            pl.ds(pl.multiple_of(512 * links.x, 128), 512))


def kregion(links):
    return pl.ds(pl.multiple_of(48 * links.k, 8), 48), slice(None)


def gather_stage(links, kind, ref, region):
    view = ref.at[region]
    return exchange(links, kind, lambda j: view, lambda j: view)


def ysum_start(links, src, buf):
    return exchange(links, "y",
                    lambda j: src.at[(slice(None),) + ypiece(place(links, "y", j))],
                    lambda j: buf.at[j])


def ysum_mid(links, copies, src, buf, res):
    mine = (slice(None),) + ypiece(links.y)
    arrive(copies)
    total = src[mine]
    for j in range(1, NY):
        total = total + buf[j]
    res[mine] = total
    return gather_stage(links, "y", res, mine)


def psum_core(links, part, bufk):
    rows = pl.ds(pl.multiple_of(48 * (1 - links.k), 8), 48)
    return exchange(links, "k", lambda j: part.at[rows, :], lambda j: bufk)


def psum_x(links, copies, part, bufk, sumk, bufx):
    arrive(copies)
    rows = pl.ds(pl.multiple_of(48 * links.k, 8), 48)
    sumk[...] = part[rows, :] + bufk[...]
    return exchange(links, "x",
                    lambda j: sumk.at[:, pl.ds(pl.multiple_of(512 * place(links, "x", j), 128), 512)],
                    lambda j: bufx.at[j])


def psum_z(links, copies, sumk, bufx, sumx, bufz):
    arrive(copies)
    total = sumk[:, pl.ds(pl.multiple_of(512 * links.x, 128), 512)]
    for j in range(1, NX):
        total = total + bufx[j]
    sumx[...] = total
    return exchange(links, "z", lambda j: sumx.at[zpiece(place(links, "z", j))], lambda j: bufz.at[j])


def psum_back_z(links, copies, sumx, bufz, out):
    arrive(copies)
    total = sumx[zpiece(links.z)]
    for j in range(1, NZ):
        total = total + bufz[j]
    region = zregion(links)
    out[region] = total
    return gather_stage(links, "z", out, region)


def factor_block(b, carry):
    w, v, e, low = carry
    row = lax.broadcasted_iota(jnp.int32, (B, 128), 0)
    lane = lax.broadcasted_iota(jnp.int32, (B, 128), 1)
    alive = row < B - 8 * b
    for s in range(8):
        d = w[s:s + 1, s:s + 1]
        rs = lax.rsqrt(d)
        rs = rs * (1.5 - 0.5 * d * rs * rs)
        rs = rs * (1.5 - 0.5 * d * rs * rs)
        col = jnp.where(alive & (row >= s), jnp.broadcast_to(w[:, s:s + 1], (B, 128)) * rs, 0.0)
        below = jnp.where(row > s, col, 0.0)
        w = w - below * (w[s:s + 1, :] * rs)
        low = jnp.where(lane == s, col, low)
        erow = e[s:s + 1, :] * rs
        e = jnp.where(row == s, jnp.broadcast_to(erow, (B, 128)), e - below * erow)
        vcol = jnp.broadcast_to(v[:, s:s + 1], (B, 128)) + col
        ip = 1.0 / vcol[s:s + 1, :]
        vrow = jnp.where(lane[0:1] == s, -1.0, v[s:s + 1, :]) * ip
        v = jnp.where((lane == s) | (row == s), 0.0, v) - jnp.where(row == s, 1.0, vcol) * vrow

    def turn(m):
        m = pltpu.roll(m, 120, axis=1)
        return jnp.concatenate([m[8:], m[:8]], axis=0)

    e = jnp.concatenate([e[8:], e[:8]], axis=0)
    return turn(w), turn(v), e, turn(low)


def factor(gram, top):
    row = lax.broadcasted_iota(jnp.int32, (B, 128), 0)
    lane = lax.broadcasted_iota(jnp.int32, (B, 128), 1)
    w, v, e, low = lax.fori_loop(
        0, B // 8, factor_block,
        (gram, -top, (row == lane).astype(F32), jnp.zeros((B, 128), F32)))
    return pltpu.roll(low, 96, axis=1), e, pltpu.roll(v, 96, axis=1)


def body(a_ref, o_ref, wsrc, wr, wc, stgk, stgx,
         part, bufk, sumk, bufx, sumx, bufz, yc,
         ysrc, ybuf, yres, csrc, cbuf, cres, pcs, prs, aec, aer, yy, kc, hc, sq, send, recv):
    links = Links(send, recv)
    x, z, k, y, row = links.x, links.z, links.k, links.y, links.row

    barrier = pltpu.get_barrier_semaphore()
    for kind in ("y", "x", "z", "k"):
        for j in range(1, SIZE[kind]):
            pl.semaphore_signal(barrier, inc=1, device_id=links.at(kind, j), device_id_type=MESH)
    pl.semaphore_wait(barrier, NY - 1 + NX - 1 + NZ - 1 + 1)

    lo, hi = (pl.ds(0, 1), pl.ds(1, 2))

    first = links.sems(2 * NY)

    def yscatter(j, part_, sem):
        piece = (part_,) + ypiece(j)
        return links.copy(wsrc.at[piece], wr.at[piece], first + sem, "y", j)

    @pl.when(y == 0)
    def _():
        for g in range(3):
            wsrc[g] = a_ref[:, 0:384].T[g * B:(g + 1) * B]
        wr[(slice(None),) + ypiece(0)] = wsrc[(slice(None),) + ypiece(0)]
        for j in range(1, NY):
            yscatter(j, lo, j).start()
        for j in range(1, NY):
            yscatter(j, hi, NY + j).start()

    core = links.sems(3)
    core_copies = [links.copy(a_ref.at[pl.ds(48, 48), :], stgk.at[0], core, "k", 1),
                   links.copy(a_ref.at[pl.ds(144, 48), :], stgk.at[1], core + 1, "k", 1),
                   links.copy(a_ref.at[pl.ds(240, 16), :], stgk.at[2, pl.ds(0, 16), :], core + 2, "k", 1)]

    @pl.when(row == 0)
    def _():
        for copy in core_copies:
            copy.start()
        stgk[0] = a_ref[0:48, :]
        stgk[1] = a_ref[96:144, :]
        stgk[2] = a_ref[192:240, :]

    @pl.when(row == 1)
    def _():
        stgk[2, 16:48, :] = a_ref[0:32, :]

    xs = links.sems(2 * NX)

    def xscatter(j, part_, sem):
        return links.copy(stgk.at[part_, :, pl.ds(512 * j, 512)], stgx.at[part_], xs + sem, "x", j)

    @pl.when((x == 0) & (z == 0))
    def _():
        for part_, base in ((lo, 0), (hi, NX)):
            @pl.when(k == 1)
            def _():
                for copy in (core_copies[:1] if base == 0 else core_copies[1:]):
                    copy.wait_recv()
            for j in range(1, NX):
                xscatter(j, part_, base + j).start()
        stgx[...] = stgk[:, :, 0:512]

    mine = ypiece(y)

    @pl.when(y != 0)
    def _():
        for g, part_ in enumerate((lo, hi)):
            piece = (part_,) + mine
            links.copy(wr.at[piece], wr.at[piece], first + g * NY + y, "y", 0).wait_recv()

    wr_lo = gather_stage(links, "y", wr, (lo,) + mine)
    wr_hi = gather_stage(links, "y", wr, (hi,) + mine)

    zs = links.sems(2 * NZ)

    def zscatter(j, part_, sem):
        rows, lanes = zpiece(j)
        to_rows = pl.ds(pl.multiple_of(48 * k + 24 * (j % 2), 8), 24)
        to_lanes = pl.ds(pl.multiple_of(512 * x + 128 * (j // 2), 128), 128)
        return links.copy(stgx.at[part_, rows, lanes], wc.at[part_, to_rows, to_lanes], zs + sem, "z", j)

    @pl.when(z == 0)
    def _():
        for part_, base in ((lo, 0), (hi, NX)):
            @pl.when(x != 0)
            def _():
                links.copy(stgx.at[part_], stgx.at[part_], xs + base + x, "x", 0).wait_recv()
            for j in range(1, NZ):
                zscatter(j, part_, (0 if base == 0 else NZ) + j).start()
        wc[(slice(None),) + zregion(links)] = stgx[(slice(None),) + zpiece(0)]

    arrive(wr_lo)

    gl_r = row * ROWS + lax.broadcasted_iota(jnp.int32, (B, ROWS), 1)
    gl_c = y * COLS + lax.broadcasted_iota(jnp.int32, (B, COLS), 1)
    lane128 = lax.broadcasted_iota(jnp.int32, (B, 128), 1)

    def product_cols(pr, mat, out):
        def step(i, _):
            lanes = pl.ds(pl.multiple_of(512 * i, 512), 512)
            out[:, lanes] = nn(pr, mat[:, lanes])
            return 0
        lax.fori_loop(0, 4, step, 0)

    def product_rows(pc, mat):
        def step(i, acc):
            lanes = pl.ds(pl.multiple_of(512 * i, 512), 512)
            return acc + nt(pc[:, lanes], mat[:, lanes])
        return lax.fori_loop(0, 4, step, jnp.zeros((B, ROWS), F32))

    def gram_of(pc, other):
        def step(i, acc):
            lanes = pl.ds(pl.multiple_of(512 * i, 512), 512)
            return acc + nt(pc[:, lanes], other[:, lanes])
        return lax.fori_loop(0, 4, step, jnp.zeros((B, B), F32))

    def widen(m):
        sq[...] = jnp.zeros((B, 128), F32)
        sq[:, 0:B] = m
        return sq[...]

    first_col = y == 0

    def unit_part(chol, trail, width):
        wide = jnp.concatenate([chol] + [jnp.zeros((B, 128), F32)] * (width // 128 - 1), axis=1)
        return pltpu.roll(wide, trail, axis=1)

    pr = jnp.where(gl_r >= B, wr[0], 0.0)
    prs[0] = pr
    product_cols(pr, a_ref, part.at[0])
    ps = psum_core(links, part.at[0], bufk.at[0])

    @pl.when(z != 0)
    def _():
        for g, part_ in enumerate((lo, hi)):
            region = (part_,) + zregion(links)
            links.copy(wc.at[region], wc.at[region], zs + g * NZ + z, "z", 0).wait_recv()

    wlo = gather_stage(links, "z", wc, (lo,) + zregion(links))
    whi = gather_stage(links, "z", wc, (hi,) + zregion(links))
    ps = psum_x(links, ps, part.at[0], bufk.at[0], sumk.at[0], bufx.at[0])
    arrive(wlo)
    wlo = gather_stage(links, "x", wc, (lo,) + xregion(links))
    ps = psum_z(links, ps, sumk.at[0], bufx.at[0], sumx.at[0], bufz.at[0])
    arrive(wlo)
    wlo = gather_stage(links, "k", wc, (lo,) + kregion(links))
    arrive(whi)
    whi = gather_stage(links, "x", wc, (hi,) + xregion(links))
    arrive(wlo)

    pcs[0] = jnp.where(gl_c >= B, wc[0], 0.0)

    def panel(p, ps, mat, wc_p, wr_p, whi):
        trail = (p + 1) * B
        pc = pcs.at[p]
        ysrc[p, 0, :, 0:128] = widen(gram_of(pc, pc))
        ysrc[p, 0, :, 128:256] = jnp.where(first_col, pc[:, 0:128], 0.0)
        ysrc[p, 1] = jnp.where(first_col, pc[:, 128:384], 0.0)
        ysrc[p, 2] = product_rows(pc, mat)
        ys = ysum_start(links, ysrc.at[p], ybuf.at[p])
        ps = psum_back_z(links, ps, sumx.at[p], bufz.at[p], yc.at[p])
        ys = ysum_mid(links, ys, ysrc.at[p], ybuf.at[p], yres.at[p])
        arrive(ps)
        ps = gather_stage(links, "x", yc.at[p], xregion(links))
        if whi is not None:
            arrive(whi)
            whi = gather_stage(links, "k", wc, (hi,) + kregion(links))
        arrive(ys)
        gram = yres[p, 0, :, 0:128]
        pwin = jnp.concatenate([yres[p, 0, :, 128:256], yres[p, 1]], axis=1)
        top = jnp.where(lane128 < B, pltpu.roll(pwin, 384 - trail, axis=1)[:, 0:128], 0.0)
        chol, chol_inv, v = factor(gram, top)
        arrive(ps)
        ps = gather_stage(links, "k", yc.at[p], kregion(links))
        nt_ = nn(v.T[0:B], chol_inv)[:, 0:B]
        low = chol[:, 0:B]
        unit = unit_part(chol, trail, 512)
        kc[...] = -pc[...]
        kc[:, 0:512] = kc[:, 0:512] + jnp.where(first_col, unit, 0.0)
        arrive(ps)
        if whi is not None:
            arrive(whi)

        def make_y(i, _):
            lanes = pl.ds(pl.multiple_of(512 * i, 512), 512)
            yy[:, lanes] = nn(low, wc_p[:, lanes]) - yc[p, :, lanes]
            return 0
        lax.fori_loop(0, 4, make_y, 0)
        csrc[p, 0, :, 0:128] = widen(gram_of(kc, yy))
        csrc[p, 0, :, 128:256] = jnp.where(first_col, yy[:, 0:128], 0.0)
        csrc[p, 1] = jnp.where(first_col, yy[:, 128:384], 0.0)
        cs = ysum_start(links, csrc.at[p], cbuf.at[p])
        kr = (jnp.where(row == 0, unit[:, 0:256], 0.0) + jnp.where(row == 1, unit[:, 256:512], 0.0)) - prs[p]
        yr = nn(low, wr_p[...]) - yres[p, 2]
        nty = nn(nt_, yr)
        cs = ysum_mid(links, cs, csrc.at[p], cbuf.at[p], cres.at[p])
        arrive(cs)
        c = cres[p, 0, :, 0:B]
        nd = -0.5 * nt(nn(nt_, c), nt_)
        hr = nty + nn(nd, kr)

        def make_h(i, _):
            lanes = pl.ds(pl.multiple_of(512 * i, 512), 512)
            hc[:, lanes] = nn(nt_, yy[:, lanes]) + nn(nd, kc[:, lanes])
            return 0
        lax.fori_loop(0, 4, make_h, 0)
        left = jnp.concatenate([hr, kr], axis=0).T

        def update(i, _):
            lanes = pl.ds(pl.multiple_of(512 * i, 512), 512)
            right = jnp.concatenate([kc[:, lanes], hc[:, lanes]], axis=0)
            o_ref[:, lanes] = mat[:, lanes] - nn(left, right)
            return 0

        if p == 1:
            lax.fori_loop(0, 4, update, 0)
            return None

        ywin = jnp.concatenate([cres[p, 0, :, 128:256], cres[p, 1]], axis=1)
        kwin = unit[:, 0:384] - pwin
        hwin = nn(nt_, ywin) + nn(nd, kwin)
        rows = jnp.concatenate([hwin, kwin], axis=0).T[B:3 * B]
        new = nn(rows, jnp.concatenate([kr, hr], axis=0))
        prs[1] = jnp.where(gl_r >= 2 * B, wr[1] - new[0:B], 0.0)
        aer[...] = wr[2] - new[B:]

        def next_rows(i, _):
            lanes = pl.ds(pl.multiple_of(512 * i, 512), 512)
            right = jnp.concatenate([kc[:, lanes], hc[:, lanes]], axis=0)
            fresh = nn(rows, right)
            pcs[1, :, lanes] = wc[1, :, lanes] - fresh[0:B]
            aec[:, lanes] = wc[2, :, lanes] - fresh[B:]
            return 0

        lax.fori_loop(0, 4, update, 0)
        product_cols(prs[1], o_ref, part.at[1])
        ps = psum_core(links, part.at[1], bufk.at[1])
        lax.fori_loop(0, 4, next_rows, 0)
        pcs[1] = jnp.where(gl_c >= 2 * B, pcs[1], 0.0)
        ps = psum_x(links, ps, part.at[1], bufk.at[1], sumk.at[1], bufx.at[1])
        return psum_z(links, ps, sumk.at[1], bufx.at[1], sumx.at[1], bufz.at[1])

    arrive(wr_hi)
    ps = panel(0, ps, a_ref, wc.at[1], wr.at[1], whi)
    panel(1, ps, o_ref, aec, aer, None)

    @pl.when(y == 0)
    def _():
        for j in range(1, NY):
            yscatter(j, lo, j).wait_send()
            yscatter(j, hi, NY + j).wait_send()

    @pl.when(row == 0)
    def _():
        for copy in core_copies:
            copy.wait_send()

    @pl.when((x == 0) & (z == 0))
    def _():
        for j in range(1, NX):
            xscatter(j, lo, j).wait_send()
            xscatter(j, hi, NX + j).wait_send()

    @pl.when(z == 0)
    def _():
        for j in range(1, NZ):
            zscatter(j, lo, j).wait_send()
            zscatter(j, hi, NZ + j).wait_send()

    links.finish()


def local(matrix):
    vmem = pltpu.VMEM
    return pl.pallas_call(
        body,
        out_shape=jax.ShapeDtypeStruct((ROWS, COLS), F32),
        in_specs=[pl.BlockSpec(memory_space=pltpu.VMEM)],
        out_specs=pl.BlockSpec(memory_space=pltpu.VMEM),
        scratch_shapes=[
            vmem((3, B, ROWS), F32), vmem((3, B, ROWS), F32), vmem((3, B, COLS), F32),
            vmem((3, 48, COLS), F32), vmem((3, 48, 512), F32),
            vmem((2, B, COLS), F32), vmem((2, 48, COLS), F32), vmem((2, 48, COLS), F32),
            vmem((2, NX, 48, 512), F32), vmem((2, 48, 512), F32), vmem((2, NZ, 24, 128), F32), vmem((2, B, COLS), F32),
            vmem((2, 3, B, 256), F32), vmem((2, NY, 3, 24, 128), F32), vmem((2, 3, B, 256), F32),
            vmem((2, 2, B, 256), F32), vmem((2, NY, 2, 24, 128), F32), vmem((2, 2, B, 256), F32),
            vmem((2, B, COLS), F32), vmem((2, B, ROWS), F32), vmem((B, COLS), F32), vmem((B, ROWS), F32),
            vmem((B, COLS), F32), vmem((B, COLS), F32), vmem((B, COLS), F32), vmem((B, 128), F32),
            pltpu.SemaphoreType.DMA((SEND_SEMS,)), pltpu.SemaphoreType.DMA((SEND_SEMS,)),
        ],
        compiler_params=pltpu.CompilerParams(
            collective_id=0, has_side_effects=True, vmem_limit_bytes=56 * 1024 * 1024),
        name="two_panels",
    )(matrix)


def solution(mesh):
    return jax.shard_map(local, mesh=mesh, in_specs=(P("row", "col"),), out_specs=P("row", "col"), check_vma=False)
```

```python
import jax
import jax.numpy as jnp
from jax import lax
from jax.experimental import pallas as pl
from jax.experimental.pallas import tpu as pltpu
from jax.sharding import PartitionSpec as P

B = 96
ROWS = 256
COLS = 2048
NX, NZ, NY = 4, 8, 8
F32 = jnp.float32
HIGH = lax.Precision.HIGHEST
MESH = pl.DeviceIdType.MESH

SEND_SEMS = 320


def nn(a, b):
    return lax.dot_general(a, b, (((1,), (0,)), ((), ())), precision=HIGH, preferred_element_type=F32)


def nt(a, b):
    return lax.dot_general(a, b, (((1,), (1,)), ((), ())), precision=HIGH, preferred_element_type=F32)


class Links:
    def __init__(self, send, recv):
        self.send, self.recv, self.count, self.open = send, recv, 0, []
        row, self.y = lax.axis_index("row"), lax.axis_index("col")
        self.row = row
        self.x, self.z, self.k = row // 16, (row // 2) % 8, row % 2

    def sems(self, n):
        first = self.count
        self.count += n
        return first

    def at(self, kind, j):
        x, z, k, y = self.x, self.z, self.k, self.y
        if kind == "x":
            x = (x + j) % NX
        elif kind == "z":
            z = (z + j) % NZ
        elif kind == "k":
            k = (k + j) % 2
        else:
            y = (y + j) % NY
        return (x * 16 + z * 2 + k, y)

    def copy(self, src, dst, sem, kind, j):
        return pltpu.make_async_remote_copy(
            src_ref=src, dst_ref=dst, send_sem=self.send.at[sem], recv_sem=self.recv.at[sem],
            device_id=self.at(kind, j), device_id_type=MESH)

    def finish(self):
        for copy in self.open:
            copy.wait_send()


SIZE = {"x": NX, "z": NZ, "y": NY, "k": 2}


def exchange(links, kind, src_of, dst_of):
    n = SIZE[kind]
    first = links.sems(n)
    copies = []
    for j in range(1, n):
        copy = links.copy(src_of(j), dst_of(j), first + j, kind, j)
        copy.start()
        copies.append(copy)
    links.open += copies
    return copies


def arrive(copies):
    for copy in copies:
        copy.wait_recv()


def place(links, kind, j):
    return (getattr(links, kind) + j) % SIZE[kind]


def ypiece(j):
    return pl.ds(pl.multiple_of(24 * (j // 2), 8), 24), pl.ds(pl.multiple_of(128 * (j % 2), 128), 128)


def zpiece(j):
    return ypiece_rows(j), pl.ds(pl.multiple_of(128 * (j // 2), 128), 128)


def ypiece_rows(j):
    return pl.ds(pl.multiple_of(24 * (j % 2), 8), 24)


def zregion(links):
    return (pl.ds(pl.multiple_of(48 * links.k + 24 * (links.z % 2), 8), 24),
            pl.ds(pl.multiple_of(512 * links.x + 128 * (links.z // 2), 128), 128))


def xregion(links):
    return (pl.ds(pl.multiple_of(48 * links.k, 8), 48),
            pl.ds(pl.multiple_of(512 * links.x, 128), 512))


def kregion(links):
    return pl.ds(pl.multiple_of(48 * links.k, 8), 48), slice(None)


def gather_stage(links, kind, ref, region):
    view = ref.at[region]
    return exchange(links, kind, lambda j: view, lambda j: view)


def ysum_start(links, src, buf):
    return exchange(links, "y",
                    lambda j: src.at[(slice(None),) + ypiece(place(links, "y", j))],
                    lambda j: buf.at[j])


def ysum_mid(links, copies, src, buf, res):
    mine = (slice(None),) + ypiece(links.y)
    arrive(copies)
    total = src[mine]
    for j in range(1, NY):
        total = total + buf[j]
    res[mine] = total
    return gather_stage(links, "y", res, mine)


def psum_core(links, part, bufk):
    rows = pl.ds(pl.multiple_of(48 * (1 - links.k), 8), 48)
    return exchange(links, "k", lambda j: part.at[rows, :], lambda j: bufk)


def psum_x(links, copies, part, bufk, sumk, bufx):
    arrive(copies)
    rows = pl.ds(pl.multiple_of(48 * links.k, 8), 48)
    sumk[...] = part[rows, :] + bufk[...]
    return exchange(links, "x",
                    lambda j: sumk.at[:, pl.ds(pl.multiple_of(512 * place(links, "x", j), 128), 512)],
                    lambda j: bufx.at[j])


def psum_z(links, copies, sumk, bufx, sumx, bufz):
    arrive(copies)
    total = sumk[:, pl.ds(pl.multiple_of(512 * links.x, 128), 512)]
    for j in range(1, NX):
        total = total + bufx[j]
    sumx[...] = total
    return exchange(links, "z", lambda j: sumx.at[zpiece(place(links, "z", j))], lambda j: bufz.at[j])


def psum_back_z(links, copies, sumx, bufz, out):
    arrive(copies)
    total = sumx[zpiece(links.z)]
    for j in range(1, NZ):
        total = total + bufz[j]
    region = zregion(links)
    out[region] = total
    return gather_stage(links, "z", out, region)


def small_core(links, src, bufk):
    rows = pl.ds(pl.multiple_of(48 * (1 - links.k), 8), 48)
    return exchange(links, "k", lambda j: src.at[rows, :], lambda j: bufk)


def small_x(links, copies, src, bufk, parts):
    arrive(copies)
    parts[links.x] = src[pl.ds(pl.multiple_of(48 * links.k, 8), 48), :] + bufk[...]
    view = parts.at[links.x]
    return exchange(links, "x", lambda j: view, lambda j: view)


def small_z(links, copies, xparts, parts):
    arrive(copies)
    total = xparts[0]
    for j in range(1, NX):
        total = total + xparts[j]
    parts[links.z] = total
    view = parts.at[links.z]
    return exchange(links, "z", lambda j: view, lambda j: view)


def small_back(links, copies, zparts, out):
    arrive(copies)
    total = zparts[0]
    for j in range(1, NZ):
        total = total + zparts[j]
    out[kregion(links)] = total
    return gather_stage(links, "k", out, kregion(links))


def factor_block(b, carry):
    w, v, e, low = carry
    row = lax.broadcasted_iota(jnp.int32, (B, 128), 0)
    lane = lax.broadcasted_iota(jnp.int32, (B, 128), 1)
    lane1 = lane[0:1]
    alive = row < B - 8 * b
    for first in range(0, 8, 4):
        steps = range(first, first + 4)
        wcol = [jnp.broadcast_to(w[:, s:s + 1], (B, 128)) for s in steps]
        vcol = [jnp.broadcast_to(v[:, s:s + 1], (B, 128)) for s in steps]
        wrow = [w[s:s + 1, :] for s in steps]
        vrow = [v[s:s + 1, :] for s in steps]
        erow = [e[s:s + 1, :] for s in steps]
        for i, s in enumerate(steps):
            rs = lax.rsqrt(wcol[i][s:s + 1, :])
            col = jnp.where(alive & (row >= s), wcol[i] * rs, 0.0)
            wr = wrow[i] * rs
            er = erow[i] * rs
            vc = vcol[i] + col
            ip = 1.0 / vc[s:s + 1, :]
            vr = jnp.where(lane1 == s, -1.0, vrow[i]) * ip
            vm = jnp.where(row == s, 1.0, vc)
            for j in range(i + 1, 4):
                t = first + j
                cj = col[t:t + 1, :]
                wcol[j] = wcol[j] - col * cj
                wrow[j] = wrow[j] - cj * wr
                erow[j] = erow[j] - cj * er
                vj = vcol[j][s:s + 1, :] * ip
                vcol[j] = jnp.where(row == s, 0.0, vcol[j]) - vm * vj
                vrow[j] = jnp.where(lane1 == s, 0.0, vrow[j]) - vm[t:t + 1, :] * vr
            w = w - col * wr
            low = jnp.where(lane == s, col, low)
            e = jnp.where(row == s, jnp.broadcast_to(er, (B, 128)), e - jnp.where(row > s, col, 0.0) * er)
            v = jnp.where((lane == s) | (row == s), 0.0, v) - vm * vr

    def turn(m):
        m = pltpu.roll(m, 120, axis=1)
        return jnp.concatenate([m[8:], m[:8]], axis=0)

    e = jnp.concatenate([e[8:], e[:8]], axis=0)
    return turn(w), turn(v), e, turn(low)


def factor_start(gram, top):
    row = lax.broadcasted_iota(jnp.int32, (B, 128), 0)
    lane = lax.broadcasted_iota(jnp.int32, (B, 128), 1)
    return gram, -top, (row == lane).astype(F32), jnp.zeros((B, 128), F32)


def factor_some(first, last, state):
    return lax.fori_loop(first, last, factor_block, state)


def factor_end(state):
    _, v, e, low = state
    low = pltpu.roll(low, 96, axis=1)[:, 0:B]
    v = pltpu.roll(v, 96, axis=1)
    return low, nn(v.T[0:B], e)[:, 0:B]


def body(a_ref, o_ref, wsrc, wr, wc, stgk, stgx,
         part, bufk, sumk, bufx, sumx, bufz, yc,
         gsrc, gbuf, gres, rsrc, rbuf, rres, csrc, cbuf, cres, esrc, ebuf, eres,
         ssrc, sbufk, sx, sz, sres,
         pcs, prs, aec, aer, yy, kc, hc, sq, send, recv):
    links = Links(send, recv)
    x, z, k, y, row = links.x, links.z, links.k, links.y, links.row

    barrier = pltpu.get_barrier_semaphore()
    for kind in ("y", "x", "z", "k"):
        for j in range(1, SIZE[kind]):
            pl.semaphore_signal(barrier, inc=1, device_id=links.at(kind, j), device_id_type=MESH)

    @pl.when(y == 0)
    def _():
        wsrc[0] = a_ref[:, 0:128].T[0:B]

    pl.semaphore_wait(barrier, NY - 1 + NX - 1 + NZ - 1 + 1)

    lo, hi = (pl.ds(0, 1), pl.ds(1, 2))
    origin = (x == 0) & (z == 0)

    ysc = links.sems(2 * NY)
    core = links.sems(3)
    xsc = links.sems(2 * NX)
    zsc = links.sems(2 * NZ)
    mine = ypiece(y)

    def yscatter(j, part_, sem):
        piece = (part_,) + ypiece(j)
        return links.copy(wsrc.at[piece], wr.at[piece], ysc + sem, "y", j)

    core_copies = [links.copy(a_ref.at[pl.ds(48, 48), :], stgk.at[0], core, "k", 1),
                   links.copy(a_ref.at[pl.ds(144, 48), :], stgk.at[1], core + 1, "k", 1),
                   links.copy(a_ref.at[pl.ds(240, 16), :], stgk.at[2, pl.ds(0, 16), :], core + 2, "k", 1)]

    def xscatter(j, part_, sem):
        return links.copy(stgk.at[part_, :, pl.ds(512 * j, 512)], stgx.at[part_], xsc + sem, "x", j)

    def zscatter(j, part_, sem):
        rows, lanes = zpiece(j)
        to_rows = pl.ds(pl.multiple_of(48 * k + 24 * (j % 2), 8), 24)
        to_lanes = pl.ds(pl.multiple_of(512 * x + 128 * (j // 2), 128), 128)
        return links.copy(stgx.at[part_, rows, lanes], wc.at[part_, to_rows, to_lanes], zsc + sem, "z", j)

    def y_out(part_, g):
        @pl.when(y == 0)
        def _():
            wr[(part_,) + ypiece(0)] = wsrc[(part_,) + ypiece(0)]
            for j in range(1, NY):
                yscatter(j, part_, g * NY + j).start()

    def y_in(part_, g):
        piece = (part_,) + mine

        @pl.when(y != 0)
        def _():
            links.copy(wr.at[piece], wr.at[piece], ysc + g * NY + y, "y", 0).wait_recv()

        return gather_stage(links, "y", wr, piece)

    def x_out(part_, g):
        @pl.when(origin)
        def _():
            @pl.when(k == 1)
            def _():
                for copy in (core_copies[:1] if g == 0 else core_copies[1:]):
                    copy.wait_recv()
            for j in range(1, NX):
                xscatter(j, part_, g * NX + j).start()
            stgx[part_] = stgk[part_, :, 0:512]

    def z_out(part_, g):
        @pl.when(z == 0)
        def _():
            @pl.when(x != 0)
            def _():
                links.copy(stgx.at[part_], stgx.at[part_], xsc + g * NX + x, "x", 0).wait_recv()
            for j in range(1, NZ):
                zscatter(j, part_, g * NZ + j).start()
            wc[(part_,) + zregion(links)] = stgx[(part_,) + zpiece(0)]

    def z_in(part_, g):
        region = (part_,) + zregion(links)

        @pl.when(z != 0)
        def _():
            links.copy(wc.at[region], wc.at[region], zsc + g * NZ + z, "z", 0).wait_recv()

        return gather_stage(links, "z", wc, region)

    y_out(lo, 0)

    @pl.when(row == 0)
    def _():
        core_copies[0].start()
        stgk[0] = a_ref[0:48, :]

    x_out(lo, 0)
    wr_lo = y_in(lo, 0)

    @pl.when(row == 0)
    def _():
        for copy in core_copies[1:]:
            copy.start()
        stgk[1] = a_ref[96:144, :]
        stgk[2] = a_ref[192:240, :]

    @pl.when(row == 1)
    def _():
        stgk[2, 16:48, :] = a_ref[0:32, :]

    @pl.when(y == 0)
    def _():
        t = a_ref[:, 0:384].T
        wsrc[1] = t[B:2 * B]
        wsrc[2] = t[2 * B:3 * B]

    z_out(lo, 0)
    y_out(hi, 1)

    gl_r = row * ROWS + lax.broadcasted_iota(jnp.int32, (B, ROWS), 1)
    gl_c = y * COLS + lax.broadcasted_iota(jnp.int32, (B, COLS), 1)
    lane128 = lax.broadcasted_iota(jnp.int32, (B, 128), 1)
    first_col = y == 0

    def chunks(step):
        def run(i, _):
            step(pl.ds(pl.multiple_of(512 * i, 512), 512))
            return 0
        lax.fori_loop(0, 4, run, 0)

    def product_cols(pr, mat, out):
        def step(lanes):
            out[:, lanes] = nn(pr, mat[:, lanes])
        chunks(step)

    def product_rows(pc, mat, width):
        def step(i, acc):
            lanes = pl.ds(pl.multiple_of(512 * i, 512), 512)
            return acc + nt(pc[:, lanes], mat[:, lanes])
        return lax.fori_loop(0, 4, step, jnp.zeros((B, width), F32))

    def widen(m):
        sq[...] = jnp.zeros((B, 128), F32)
        sq[:, 0:B] = m
        return sq[...]

    def square(window, at):
        width = window.shape[1]
        return jnp.where(lane128 < B, pltpu.roll(window, width - at, axis=1)[:, 0:128], 0.0)

    def col_square(ref, at):
        return jnp.where(first_col, square(ref[:, 0:384], at), 0.0)

    def unit_part(chol, trail):
        wide = jnp.concatenate([widen(chol), jnp.zeros((B, 384), F32)], axis=1)
        return pltpu.roll(wide, trail, axis=1)

    def make_k(unit, p):
        kc[...] = -pcs[p]
        kc[:, 0:512] = kc[:, 0:512] + jnp.where(first_col, unit, 0.0)
        return (jnp.where(row == 0, unit[:, 0:256], 0.0) + jnp.where(row == 1, unit[:, 256:512], 0.0)) - prs[p]

    arrive(wr_lo)
    prs[0] = jnp.where(gl_r >= B, wr[0], 0.0)
    product_cols(prs[0], a_ref, part.at[0])
    ps = psum_core(links, part.at[0], bufk.at[0])
    wlo = z_in(lo, 0)
    ps = psum_x(links, ps, part.at[0], bufk.at[0], sumk.at[0], bufx.at[0])
    x_out(hi, 1)
    wr_hi = y_in(hi, 1)
    arrive(wlo)
    wlo = gather_stage(links, "x", wc, (lo,) + xregion(links))
    ps = psum_z(links, ps, sumk.at[0], bufx.at[0], sumx.at[0], bufz.at[0])
    arrive(wlo)
    wlo = gather_stage(links, "k", wc, (lo,) + kregion(links))
    z_out(hi, 1)
    arrive(wlo)
    pcs[0] = jnp.where(gl_c >= B, wc[0], 0.0)
    gsrc[0, 0, :, 0:128] = widen(product_rows(pcs.at[0], pcs.at[0], B))
    gsrc[0, 0, :, 128:256] = col_square(pcs.at[0], B)
    gs = ysum_start(links, gsrc.at[0], gbuf.at[0])
    whi = z_in(hi, 1)
    ps = psum_back_z(links, ps, sumx.at[0], bufz.at[0], yc.at[0])
    rsrc[0, 0] = product_rows(pcs.at[0], a_ref, ROWS)
    gs = ysum_mid(links, gs, gsrc.at[0], gbuf.at[0], gres.at[0])
    rs = ysum_start(links, rsrc.at[0], rbuf.at[0])
    arrive(ps)
    ps = gather_stage(links, "x", yc.at[0], xregion(links))
    arrive(whi)
    whi = gather_stage(links, "x", wc, (hi,) + xregion(links))
    arrive(gs)
    top = gres[0, 0, :, 128:256]
    state = factor_start(gres[0, 0, :, 0:128], top)
    arrive(ps)
    ps = gather_stage(links, "k", yc.at[0], kregion(links))
    state = factor_some(0, 4, state)
    arrive(whi)
    whi = gather_stage(links, "k", wc, (hi,) + kregion(links))
    arrive(ps)
    arrive(whi)
    csrc[0, 0, :, 0:128] = widen(product_rows(pcs.at[0], yc.at[0], B))
    csrc[0, 0, :, 128:256] = col_square(yc.at[0], B)
    csrc[0, 1, :, 0:128] = col_square(wc.at[1], B)
    csrc[0, 1, :, 128:256] = col_square(yc.at[0], 2 * B)
    cs = ysum_start(links, csrc.at[0], cbuf.at[0])
    rs = ysum_mid(links, rs, rsrc.at[0], rbuf.at[0], rres.at[0])
    state = factor_some(4, 8, state)
    cs = ysum_mid(links, cs, csrc.at[0], cbuf.at[0], cres.at[0])
    esrc[0, :, 0:128] = col_square(wc.at[0], 2 * B)
    esrc[0, :, 128:256] = col_square(wc.at[1], 2 * B)
    esrc[1, :, 0:128] = col_square(wc.at[2], 2 * B)
    esrc[1, :, 128:256] = jnp.zeros((B, 128), F32)
    es = ysum_start(links, esrc, ebuf)
    state = factor_some(8, 12, state)
    low, nt_ = factor_end(state)
    unit = unit_part(low, B)
    kr = make_k(unit, 0)

    def image(lanes):
        yy[:, lanes] = nn(low, wc[1, :, lanes]) - yc[0, :, lanes]
    chunks(image)
    arrive(rs)
    arrive(wr_hi)
    yr = nn(low, wr[1]) - rres[0, 0]
    es = ysum_mid(links, es, esrc, ebuf, eres)
    arrive(cs)

    def coupling(low, nt_, att, yt, phi):
        head = nn(low, att) - yt
        c = nt(head, low) - nt(low, yt) + phi
        return head, -0.5 * nt(nn(nt_, c), nt_)

    head, nd = coupling(low, nt_, cres[0, 1, :, 0:B], cres[0, 0, :, 128:128 + B], cres[0, 0, :, 0:B])
    kt = low - top[:, 0:B]
    ht = nn(nt_, head) + nn(nd, kt)
    rows1 = jnp.concatenate([ht, kt], axis=0).T

    def next_panel(lanes):
        hcl = nn(nt_, yy[:, lanes]) + nn(nd, kc[:, lanes])
        hc[:, lanes] = hcl
        fresh = wc[1, :, lanes] - nn(rows1, jnp.concatenate([kc[:, lanes], hcl], axis=0))
        pcs[1, :, lanes] = fresh
    chunks(next_panel)
    pcs[1] = jnp.where(gl_c >= 2 * B, pcs[1], 0.0)
    gsrc[1, 0, :, 0:128] = widen(product_rows(pcs.at[1], pcs.at[1], B))
    gsrc[1, 0, :, 128:256] = col_square(pcs.at[1], 2 * B)
    gs = ysum_start(links, gsrc.at[1], gbuf.at[1])
    hr = nn(nt_, yr) + nn(nd, kr)
    right_r = jnp.concatenate([kr, hr], axis=0)
    prs[1] = jnp.where(gl_r >= 2 * B, wr[1] - nn(rows1, right_r), 0.0)
    left = jnp.concatenate([hr, kr], axis=0).T

    def update(lanes):
        right = jnp.concatenate([kc[:, lanes], hc[:, lanes]], axis=0)
        o_ref[:, lanes] = a_ref[:, lanes] - nn(left, right)
    chunks(update)

    rsrc[1, 0] = product_rows(pcs.at[1], o_ref, ROWS)
    rs = ysum_start(links, rsrc.at[1], rbuf.at[1])
    product_cols(prs[1], o_ref, part.at[1])
    ps = psum_core(links, part.at[1], bufk.at[1])
    gs = ysum_mid(links, gs, gsrc.at[1], gbuf.at[1], gres.at[1])
    ps = psum_x(links, ps, part.at[1], bufk.at[1], sumk.at[1], bufx.at[1])
    arrive(es)
    kt = -eres[0, :, 0:B]
    ht = nn(nt_, nn(low, eres[0, :, 128:128 + B]) - cres[0, 1, :, 128:128 + B]) + nn(nd, kt)
    rows2 = jnp.concatenate([ht, kt], axis=0).T
    att = eres[1, :, 0:B] - nn(rows2, jnp.concatenate([kt, ht], axis=0))
    aer[...] = wr[2] - nn(rows2, right_r)
    rs = ysum_mid(links, rs, rsrc.at[1], rbuf.at[1], rres.at[1])

    def next_rows(lanes):
        aec[:, lanes] = wc[2, :, lanes] - nn(rows2, jnp.concatenate([kc[:, lanes], hc[:, lanes]], axis=0))
    chunks(next_rows)
    ps = psum_z(links, ps, sumk.at[1], bufx.at[1], sumx.at[1], bufz.at[1])
    arrive(gs)
    top = gres[1, 0, :, 128:256]
    state = factor_some(0, 6, factor_start(gres[1, 0, :, 0:128], top))
    arrive(rs)
    yrow = rres[1, 0]
    none = jnp.zeros((B, ROWS), F32)
    ssrc[:, 0:128] = widen(nt(prs[1], yrow))
    ssrc[:, 128:256] = (jnp.where(row == 0, square(jnp.concatenate([yrow, none], axis=1), 2 * B), 0.0)
                        + jnp.where(row == 1, square(jnp.concatenate([none, yrow], axis=1), 2 * B), 0.0))
    ss = small_core(links, ssrc, sbufk)
    state = factor_some(6, 8, state)
    ss = small_x(links, ss, ssrc, sbufk, sx)
    ps = psum_back_z(links, ps, sumx.at[1], bufz.at[1], yc.at[1])
    state = factor_some(8, 12, state)
    ss = small_z(links, ss, sx, sz)
    low, nt_ = factor_end(state)
    kr = make_k(unit_part(low, 2 * B), 1)
    yr = nn(low, aer[...]) - yrow
    nty = nn(nt_, yr)
    arrive(ps)
    ps = gather_stage(links, "x", yc.at[1], xregion(links))

    def image_free(lanes):
        yy[:, lanes] = nn(low, aec[:, lanes])
    chunks(image_free)
    arrive(ps)
    ps = gather_stage(links, "k", yc.at[1], kregion(links))
    ss = small_back(links, ss, sz, sres)
    arrive(ps)
    arrive(ss)
    head, nd = coupling(low, nt_, att, sres[:, 128:128 + B], sres[:, 0:B])
    left = jnp.concatenate([nty + nn(nd, kr), kr], axis=0).T

    def last(lanes):
        kcl = kc[:, lanes]
        hcl = nn(nt_, yy[:, lanes] - yc[1, :, lanes]) + nn(nd, kcl)
        o_ref[:, lanes] = o_ref[:, lanes] - nn(left, jnp.concatenate([kcl, hcl], axis=0))
    chunks(last)

    @pl.when(y == 0)
    def _():
        for j in range(1, NY):
            yscatter(j, lo, j).wait_send()
            yscatter(j, hi, NY + j).wait_send()

    @pl.when(row == 0)
    def _():
        for copy in core_copies:
            copy.wait_send()

    @pl.when(origin)
    def _():
        for j in range(1, NX):
            xscatter(j, lo, j).wait_send()
            xscatter(j, hi, NX + j).wait_send()

    @pl.when(z == 0)
    def _():
        for j in range(1, NZ):
            zscatter(j, lo, j).wait_send()
            zscatter(j, hi, NZ + j).wait_send()

    links.finish()


def local(matrix):
    vmem = pltpu.VMEM

    def ysum_buffers(lead, n):
        return [vmem(lead + (n, B, 256), F32), vmem(lead + (NY, n, 24, 128), F32), vmem(lead + (n, B, 256), F32)]

    return pl.pallas_call(
        body,
        out_shape=jax.ShapeDtypeStruct((ROWS, COLS), F32),
        in_specs=[pl.BlockSpec(memory_space=pltpu.VMEM)],
        out_specs=pl.BlockSpec(memory_space=pltpu.VMEM),
        scratch_shapes=[
            vmem((3, B, ROWS), F32), vmem((3, B, ROWS), F32), vmem((3, B, COLS), F32),
            vmem((3, 48, COLS), F32), vmem((3, 48, 512), F32),
            vmem((2, B, COLS), F32), vmem((2, 48, COLS), F32), vmem((2, 48, COLS), F32),
            vmem((2, NX, 48, 512), F32), vmem((2, 48, 512), F32), vmem((2, NZ, 24, 128), F32), vmem((2, B, COLS), F32),
            *ysum_buffers((2,), 1), *ysum_buffers((2,), 1), *ysum_buffers((1,), 2), *ysum_buffers((), 2),
            vmem((B, 256), F32), vmem((48, 256), F32), vmem((NX, 48, 256), F32), vmem((NZ, 48, 256), F32), vmem((B, 256), F32),
            vmem((2, B, COLS), F32), vmem((2, B, ROWS), F32), vmem((B, COLS), F32), vmem((B, ROWS), F32),
            vmem((B, COLS), F32), vmem((B, COLS), F32), vmem((B, COLS), F32), vmem((B, 128), F32),
            pltpu.SemaphoreType.DMA((SEND_SEMS,)), pltpu.SemaphoreType.DMA((SEND_SEMS,)),
        ],
        compiler_params=pltpu.CompilerParams(
            collective_id=0, has_side_effects=True, vmem_limit_bytes=56 * 1024 * 1024),
        name="two_panels",
    )(matrix)


def solution(mesh):
    return jax.shard_map(local, mesh=mesh, in_specs=(P("row", "col"),), out_specs=P("row", "col"), check_vma=False)
```

```python
import jax
import jax.numpy as jnp
from jax import lax
from jax.experimental import pallas as pl
from jax.experimental.pallas import tpu as pltpu
from jax.sharding import PartitionSpec as P

B = 96
ROWS = 256
COLS = 2048
NX, NZ, NY = 4, 8, 8
F32 = jnp.float32
HIGH = lax.Precision.HIGHEST
MESH = pl.DeviceIdType.MESH

SEND_SEMS = 400


def nn(a, b):
    return lax.dot_general(a, b, (((1,), (0,)), ((), ())), precision=HIGH, preferred_element_type=F32)


def nt(a, b):
    return lax.dot_general(a, b, (((1,), (1,)), ((), ())), precision=HIGH, preferred_element_type=F32)


class Links:
    def __init__(self, send, recv):
        self.send, self.recv, self.count, self.open = send, recv, 0, []
        row, self.y = lax.axis_index("row"), lax.axis_index("col")
        self.row = row
        self.x, self.z, self.k = row // 16, (row // 2) % 8, row % 2

    def sems(self, n):
        first = self.count
        self.count += n
        return first

    def at(self, kind, j):
        x, z, k, y = self.x, self.z, self.k, self.y
        if kind == "x":
            x = (x + j) % NX
        elif kind == "z":
            z = (z + j) % NZ
        elif kind == "k":
            k = (k + j) % 2
        else:
            y = (y + j) % NY
        return (x * 16 + z * 2 + k, y)

    def copy(self, src, dst, sem, kind, j):
        return pltpu.make_async_remote_copy(
            src_ref=src, dst_ref=dst, send_sem=self.send.at[sem], recv_sem=self.recv.at[sem],
            device_id=self.at(kind, j), device_id_type=MESH)

    def finish(self):
        for copy in self.open:
            copy.wait_send()


SIZE = {"x": NX, "z": NZ, "y": NY, "k": 2}


def exchange(links, kind, src_of, dst_of):
    n = SIZE[kind]
    first = links.sems(n)
    copies = []
    for j in range(1, n):
        copy = links.copy(src_of(j), dst_of(j), first + j, kind, j)
        copy.start()
        copies.append(copy)
    links.open += copies
    return copies


def arrive(copies):
    for copy in copies:
        copy.wait_recv()


def place(links, kind, j):
    return (getattr(links, kind) + j) % SIZE[kind]


def ypiece(j):
    return pl.ds(pl.multiple_of(24 * (j // 2), 8), 24), pl.ds(pl.multiple_of(128 * (j % 2), 128), 128)


def zpiece(j):
    return ypiece_rows(j), pl.ds(pl.multiple_of(128 * (j // 2), 128), 128)


def ypiece_rows(j):
    return pl.ds(pl.multiple_of(24 * (j % 2), 8), 24)


def zregion(links):
    return (pl.ds(pl.multiple_of(48 * links.k + 24 * (links.z % 2), 8), 24),
            pl.ds(pl.multiple_of(512 * links.x + 128 * (links.z // 2), 128), 128))


def xregion(links):
    return (pl.ds(pl.multiple_of(48 * links.k, 8), 48),
            pl.ds(pl.multiple_of(512 * links.x, 128), 512))


def kregion(links):
    return pl.ds(pl.multiple_of(48 * links.k, 8), 48), slice(None)


def gather_stage(links, kind, ref, region):
    view = ref.at[region]
    return exchange(links, kind, lambda j: view, lambda j: view)


def ysum_start(links, src, buf):
    return exchange(links, "y",
                    lambda j: src.at[(slice(None),) + ypiece(place(links, "y", j))],
                    lambda j: buf.at[j])


def ysum_mid(links, copies, src, buf, res):
    mine = (slice(None),) + ypiece(links.y)
    arrive(copies)
    total = src[mine]
    for j in range(1, NY):
        total = total + buf[j]
    res[mine] = total
    return gather_stage(links, "y", res, mine)


def psum_core(links, part, bufk):
    rows = pl.ds(pl.multiple_of(48 * (1 - links.k), 8), 48)
    return exchange(links, "k", lambda j: part.at[rows, :], lambda j: bufk)


def psum_x(links, copies, part, bufk, sumk, bufx):
    arrive(copies)
    rows = pl.ds(pl.multiple_of(48 * links.k, 8), 48)
    sumk[...] = part[rows, :] + bufk[...]
    return exchange(links, "x",
                    lambda j: sumk.at[:, pl.ds(pl.multiple_of(512 * place(links, "x", j), 128), 512)],
                    lambda j: bufx.at[j])


def psum_z(links, copies, sumk, bufx, sumx, bufz):
    arrive(copies)
    total = sumk[:, pl.ds(pl.multiple_of(512 * links.x, 128), 512)]
    for j in range(1, NX):
        total = total + bufx[j]
    sumx[...] = total
    return exchange(links, "z", lambda j: sumx.at[zpiece(place(links, "z", j))], lambda j: bufz.at[j])


def psum_back_z(links, copies, sumx, bufz, out):
    arrive(copies)
    total = sumx[zpiece(links.z)]
    for j in range(1, NZ):
        total = total + bufz[j]
    region = zregion(links)
    out[region] = total
    return gather_stage(links, "z", out, region)


def small_core(links, src, parts):
    parts[links.k] = src[ypiece(links.y)]
    view = parts.at[links.k]
    return exchange(links, "k", lambda j: view, lambda j: view)


def small_next(links, copies, kind, before, parts):
    arrive(copies)
    total = before[0]
    for j in range(1, before.shape[0]):
        total = total + before[j]
    here = getattr(links, kind)
    parts[here] = total
    view = parts.at[here]
    return exchange(links, kind, lambda j: view, lambda j: view)


def small_back(links, copies, zparts, out):
    arrive(copies)
    total = zparts[0]
    for j in range(1, NZ):
        total = total + zparts[j]
    mine = ypiece(links.y)
    out[mine] = total
    return gather_stage(links, "y", out, mine)


def factor_block(b, carry):
    w, v, e, low = carry
    row = lax.broadcasted_iota(jnp.int32, (B, 128), 0)
    lane = lax.broadcasted_iota(jnp.int32, (B, 128), 1)
    lane1 = lane[0:1]
    alive = row < B - 8 * b
    for first in range(0, 8, 4):
        steps = range(first, first + 4)
        wcol = [jnp.broadcast_to(w[:, s:s + 1], (B, 128)) for s in steps]
        vcol = [jnp.broadcast_to(v[:, s:s + 1], (B, 128)) for s in steps]
        wrow = [w[s:s + 1, :] for s in steps]
        vrow = [v[s:s + 1, :] for s in steps]
        erow = [e[s:s + 1, :] for s in steps]
        for i, s in enumerate(steps):
            rs = lax.rsqrt(wcol[i][s:s + 1, :])
            col = jnp.where(alive & (row >= s), wcol[i] * rs, 0.0)
            wr = wrow[i] * rs
            er = erow[i] * rs
            vc = vcol[i] + col
            ip = 1.0 / vc[s:s + 1, :]
            vr = jnp.where(lane1 == s, -1.0, vrow[i]) * ip
            vm = jnp.where(row == s, 1.0, vc)
            for j in range(i + 1, 4):
                t = first + j
                cj = col[t:t + 1, :]
                wcol[j] = wcol[j] - col * cj
                wrow[j] = wrow[j] - cj * wr
                erow[j] = erow[j] - cj * er
                vj = vcol[j][s:s + 1, :] * ip
                vcol[j] = jnp.where(row == s, 0.0, vcol[j]) - vm * vj
                vrow[j] = jnp.where(lane1 == s, 0.0, vrow[j]) - vm[t:t + 1, :] * vr
            w = w - col * wr
            low = jnp.where(lane == s, col, low)
            e = jnp.where(row == s, jnp.broadcast_to(er, (B, 128)), e - jnp.where(row > s, col, 0.0) * er)
            v = jnp.where((lane == s) | (row == s), 0.0, v) - vm * vr

    def turn(m):
        m = pltpu.roll(m, 120, axis=1)
        return jnp.concatenate([m[8:], m[:8]], axis=0)

    e = jnp.concatenate([e[8:], e[:8]], axis=0)
    return turn(w), turn(v), e, turn(low)


def factor_start(gram, top):
    row = lax.broadcasted_iota(jnp.int32, (B, 128), 0)
    lane = lax.broadcasted_iota(jnp.int32, (B, 128), 1)
    return gram, -top, (row == lane).astype(F32), jnp.zeros((B, 128), F32)


def factor_some(first, last, state):
    return lax.fori_loop(first, last, factor_block, state)


def factor_end(state):
    _, v, e, low = state
    low = pltpu.roll(low, 96, axis=1)[:, 0:B]
    v = pltpu.roll(v, 96, axis=1)
    return low, nn(v.T[0:B], e)[:, 0:B], e[:, 0:B]


def body(a_ref, o_ref, wsrc, wr, wc, stgk, stgx,
         part, bufk, sumk, bufx, sumx, bufz, yc,
         gsrc, gbuf, gres, rsrc, rbuf, rres, csrc, cbuf, cres, esrc, ebuf, eres, fsrc, fbuf, fres,
         ssrc, sk, sx, sz, sres,
         pcs, prs, aec, aer, yy, kc, hc, sq, send, recv):
    links = Links(send, recv)
    x, z, k, y, row = links.x, links.z, links.k, links.y, links.row

    barrier = pltpu.get_barrier_semaphore()
    for kind in ("y", "x", "z", "k"):
        for j in range(1, SIZE[kind]):
            pl.semaphore_signal(barrier, inc=1, device_id=links.at(kind, j), device_id_type=MESH)

    @pl.when(y == 0)
    def _():
        wsrc[0] = a_ref[:, 0:128].T[0:B]

    pl.semaphore_wait(barrier, NY - 1 + NX - 1 + NZ - 1 + 1)

    lo, hi = (pl.ds(0, 1), pl.ds(1, 2))
    origin = (x == 0) & (z == 0)

    ysc = links.sems(2 * NY)
    core = links.sems(3)
    xsc = links.sems(3 * NX)
    zsc = links.sems(3 * NZ)
    mine = ypiece(y)

    def yscatter(j, part_, sem):
        piece = (part_,) + ypiece(j)
        return links.copy(wsrc.at[piece], wr.at[piece], ysc + sem, "y", j)

    core_copies = [links.copy(a_ref.at[pl.ds(48, 48), :], stgk.at[0], core, "k", 1),
                   links.copy(a_ref.at[pl.ds(144, 48), :], stgk.at[1], core + 1, "k", 1),
                   links.copy(a_ref.at[pl.ds(240, 16), :], stgk.at[2, pl.ds(0, 16), :], core + 2, "k", 1)]

    def xscatter(j, g):
        return links.copy(stgk.at[g, :, pl.ds(512 * j, 512)], stgx.at[g], xsc + g * NX + j, "x", j)

    def zscatter(j, g):
        rows, lanes = zpiece(j)
        to_rows = pl.ds(pl.multiple_of(48 * k + 24 * (j % 2), 8), 24)
        to_lanes = pl.ds(pl.multiple_of(512 * x + 128 * (j // 2), 128), 128)
        return links.copy(stgx.at[g, rows, lanes], wc.at[g, to_rows, to_lanes], zsc + g * NZ + j, "z", j)

    def y_out(part_, g):
        @pl.when(y == 0)
        def _():
            wr[(part_,) + ypiece(0)] = wsrc[(part_,) + ypiece(0)]
            for j in range(1, NY):
                yscatter(j, part_, g * NY + j).start()

    def y_in(part_, g):
        piece = (part_,) + mine

        @pl.when(y != 0)
        def _():
            links.copy(wr.at[piece], wr.at[piece], ysc + g * NY + y, "y", 0).wait_recv()

        return gather_stage(links, "y", wr, piece)

    def x_out(g):
        @pl.when(origin)
        def _():
            @pl.when(k == 1)
            def _():
                core_copies[g].wait_recv()
            for j in range(1, NX):
                xscatter(j, g).start()
            stgx[g] = stgk[g, :, 0:512]

    def z_out(g):
        @pl.when(z == 0)
        def _():
            @pl.when(x != 0)
            def _():
                links.copy(stgx.at[g], stgx.at[g], xsc + g * NX + x, "x", 0).wait_recv()
            for j in range(1, NZ):
                zscatter(j, g).start()
            wc[(g,) + zregion(links)] = stgx[(g,) + zpiece(0)]

    def z_in(g):
        region = (g,) + zregion(links)

        @pl.when(z != 0)
        def _():
            links.copy(wc.at[region], wc.at[region], zsc + g * NZ + z, "z", 0).wait_recv()

        return gather_stage(links, "z", wc, region)

    y_out(lo, 0)

    @pl.when(row == 0)
    def _():
        core_copies[0].start()
        stgk[0] = a_ref[0:48, :]
        for copy in core_copies[1:]:
            copy.start()

    x_out(0)

    @pl.when(row == 0)
    def _():
        stgk[1] = a_ref[96:144, :]
        stgk[2] = a_ref[192:240, :]

    @pl.when(row == 1)
    def _():
        stgk[2, 16:48, :] = a_ref[0:32, :]

    wr_lo = y_in(lo, 0)
    x_out(1)
    x_out(2)
    z_out(0)

    gl_r = row * ROWS + lax.broadcasted_iota(jnp.int32, (B, ROWS), 1)
    gl_c = y * COLS + lax.broadcasted_iota(jnp.int32, (B, COLS), 1)
    lane128 = lax.broadcasted_iota(jnp.int32, (B, 128), 1)
    first_col = y == 0

    def chunks(step):
        def run(i, _):
            step(pl.ds(pl.multiple_of(512 * i, 512), 512))
            return 0
        lax.fori_loop(0, 4, run, 0)

    def product_cols(pr, mat, out):
        def step(lanes):
            out[:, lanes] = nn(pr, mat[:, lanes])
        chunks(step)

    def product_rows(pc, mat, width):
        def step(i, acc):
            lanes = pl.ds(pl.multiple_of(512 * i, 512), 512)
            return acc + nt(pc[:, lanes], mat[:, lanes])
        return lax.fori_loop(0, 4, step, jnp.zeros((B, width), F32))

    def widen(m):
        sq[...] = jnp.zeros((B, 128), F32)
        sq[:, 0:B] = m
        return sq[...]

    def square(window, at):
        width = window.shape[1]
        return jnp.where(lane128 < B, pltpu.roll(window, width - at, axis=1)[:, 0:128], 0.0)

    def col_square(ref, at):
        return jnp.where(first_col, square(ref[:, 0:384], at), 0.0)

    def unit_part(chol, trail):
        wide = jnp.concatenate([widen(chol), jnp.zeros((B, 384), F32)], axis=1)
        return pltpu.roll(wide, trail, axis=1)

    def make_k(unit, p):
        kc[...] = -pcs[p]
        kc[:, 0:512] = kc[:, 0:512] + jnp.where(first_col, unit, 0.0)
        return (jnp.where(row == 0, unit[:, 0:256], 0.0) + jnp.where(row == 1, unit[:, 256:512], 0.0)) - prs[p]

    arrive(wr_lo)
    prs[0] = jnp.where(gl_r >= B, wr[0], 0.0)
    product_cols(prs[0], a_ref, part.at[0])
    ps = psum_core(links, part.at[0], bufk.at[0])

    @pl.when(y == 0)
    def _():
        t = a_ref[:, 0:384].T
        wsrc[1] = t[B:2 * B]
        wsrc[2] = t[2 * B:3 * B]

    y_out(hi, 1)
    z_out(1)
    z_out(2)
    w0 = z_in(0)
    ps = psum_x(links, ps, part.at[0], bufk.at[0], sumk.at[0], bufx.at[0])
    arrive(w0)
    w0 = gather_stage(links, "x", wc, (0,) + xregion(links))
    ps = psum_z(links, ps, sumk.at[0], bufx.at[0], sumx.at[0], bufz.at[0])
    wr_hi = y_in(hi, 1)
    arrive(w0)
    w0 = gather_stage(links, "k", wc, (0,) + kregion(links))
    arrive(w0)
    pcs[0] = jnp.where(gl_c >= B, wc[0], 0.0)
    gsrc[0, 0, :, 0:128] = widen(product_rows(pcs.at[0], pcs.at[0], B))
    gsrc[0, 0, :, 128:256] = col_square(pcs.at[0], B)
    gs = ysum_start(links, gsrc.at[0], gbuf.at[0])
    ps = psum_back_z(links, ps, sumx.at[0], bufz.at[0], yc.at[0])
    rsrc[0, 0] = product_rows(pcs.at[0], a_ref, ROWS)
    gs = ysum_mid(links, gs, gsrc.at[0], gbuf.at[0], gres.at[0])
    rs = ysum_start(links, rsrc.at[0], rbuf.at[0])
    arrive(ps)
    ps = gather_stage(links, "x", yc.at[0], xregion(links))
    w1 = z_in(1)
    arrive(gs)
    top = gres[0, 0, :, 128:256]
    state = factor_some(0, 2, factor_start(gres[0, 0, :, 0:128], top))
    arrive(ps)
    ps = gather_stage(links, "k", yc.at[0], kregion(links))
    arrive(w1)
    w1 = gather_stage(links, "x", wc, (1,) + xregion(links))
    arrive(ps)
    csrc[0, 0, :, 0:128] = widen(product_rows(pcs.at[0], yc.at[0], B))
    csrc[0, 0, :, 128:256] = col_square(yc.at[0], B)
    cs = ysum_start(links, csrc.at[0], cbuf.at[0])
    rs = ysum_mid(links, rs, rsrc.at[0], rbuf.at[0], rres.at[0])
    state = factor_some(2, 6, state)
    w2 = z_in(2)
    cs = ysum_mid(links, cs, csrc.at[0], cbuf.at[0], cres.at[0])
    arrive(w1)
    w1 = gather_stage(links, "k", wc, (1,) + kregion(links))
    state = factor_some(6, 12, state)
    low, nt_, inv = factor_end(state)
    unit = unit_part(low, B)
    kr = make_k(unit, 0)
    arrive(w1)
    esrc[0, :, 0:128] = col_square(wc.at[1], B)
    esrc[0, :, 128:256] = col_square(yc.at[0], 2 * B)
    esrc[1, :, 0:128] = col_square(wc.at[0], 2 * B)
    esrc[1, :, 128:256] = col_square(wc.at[1], 2 * B)
    es = ysum_start(links, esrc, ebuf)
    arrive(rs)
    arrive(cs)

    yt, phi = cres[0, 0, :, 128:128 + B], cres[0, 0, :, 0:B]
    of_k = -nn(inv, nt(nt(yt, low) - phi, nt_))
    of_both = jnp.concatenate([inv, of_k], axis=1)

    def next_panel(lanes):
        pcs[1, :, lanes] = nn(of_both, jnp.concatenate([yc[0, :, lanes], kc[:, lanes]], axis=0))
    chunks(next_panel)
    pcs[1] = jnp.where(gl_c >= 2 * B, pcs[1], 0.0)
    gsrc[1, 0, :, 0:128] = widen(product_rows(pcs.at[1], pcs.at[1], B))
    gsrc[1, 0, :, 128:256] = col_square(pcs.at[1], 2 * B)
    gs = ysum_start(links, gsrc.at[1], gbuf.at[1])
    yrow = rres[0, 0]
    prs[1] = jnp.where(gl_r >= 2 * B, nn(of_both, jnp.concatenate([yrow, kr], axis=0)), 0.0)
    es = ysum_mid(links, es, esrc, ebuf, eres)
    arrive(w2)
    w2 = gather_stage(links, "x", wc, (2,) + xregion(links))

    def image(lanes):
        yy[:, lanes] = nn(low, wc[1, :, lanes]) - yc[0, :, lanes]
    chunks(image)
    arrive(wr_hi)
    yr = nn(low, wr[1]) - yrow

    def coupling(low, nt_, att, yt, phi):
        c = nt(nn(low, att) - yt, low) - nt(low, yt) + phi
        return -0.5 * nt(nn(nt_, c), nt_)

    arrive(es)
    nd = coupling(low, nt_, eres[0, :, 0:B], yt, phi)
    hr = nn(nt_, yr) + nn(nd, kr)
    right_r = jnp.concatenate([kr, hr], axis=0)
    left = jnp.concatenate([hr, kr], axis=0).T
    of_h = jnp.concatenate([nt_, nd], axis=1)

    def update(lanes):
        kcl = kc[:, lanes]
        hcl = nn(of_h, jnp.concatenate([yy[:, lanes], kcl], axis=0))
        hc[:, lanes] = hcl
        o_ref[:, lanes] = a_ref[:, lanes] - nn(left, jnp.concatenate([kcl, hcl], axis=0))
    chunks(update)

    rsrc[1, 0] = product_rows(pcs.at[1], o_ref, ROWS)
    rs = ysum_start(links, rsrc.at[1], rbuf.at[1])
    product_cols(prs[1], o_ref, part.at[1])
    ps = psum_core(links, part.at[1], bufk.at[1])
    gs = ysum_mid(links, gs, gsrc.at[1], gbuf.at[1], gres.at[1])
    arrive(w2)
    w2 = gather_stage(links, "k", wc, (2,) + kregion(links))
    ps = psum_x(links, ps, part.at[1], bufk.at[1], sumk.at[1], bufx.at[1])
    kt = -eres[1, :, 0:B]
    ht = nn(nt_, nn(low, eres[1, :, 128:128 + B]) - eres[0, :, 128:128 + B]) + nn(nd, kt)
    rows2 = jnp.concatenate([ht, kt], axis=0).T
    aer[...] = wr[2] - nn(rows2, right_r)
    arrive(w2)
    fsrc[0, :, 0:128] = col_square(wc.at[2], 2 * B)
    fsrc[0, :, 128:256] = jnp.zeros((B, 128), F32)
    fs = ysum_start(links, fsrc, fbuf)

    def next_rows(lanes):
        aec[:, lanes] = wc[2, :, lanes] - nn(rows2, jnp.concatenate([kc[:, lanes], hc[:, lanes]], axis=0))
    chunks(next_rows)
    rs = ysum_mid(links, rs, rsrc.at[1], rbuf.at[1], rres.at[1])
    ps = psum_z(links, ps, sumk.at[1], bufx.at[1], sumx.at[1], bufz.at[1])
    arrive(gs)
    top = gres[1, 0, :, 128:256]
    state = factor_some(0, 5, factor_start(gres[1, 0, :, 0:128], top))
    arrive(rs)
    yrow = rres[1, 0]
    none = jnp.zeros((B, ROWS), F32)
    ssrc[:, 0:128] = widen(nt(prs[1], yrow))
    ssrc[:, 128:256] = (jnp.where(row == 0, square(jnp.concatenate([yrow, none], axis=1), 2 * B), 0.0)
                        + jnp.where(row == 1, square(jnp.concatenate([none, yrow], axis=1), 2 * B), 0.0))
    ss = small_core(links, ssrc, sk)
    fs = ysum_mid(links, fs, fsrc, fbuf, fres)
    ps = psum_back_z(links, ps, sumx.at[1], bufz.at[1], yc.at[1])
    ss = small_next(links, ss, "x", sk, sx)
    state = factor_some(5, 9, state)
    ss = small_next(links, ss, "z", sx, sz)
    arrive(ps)
    ps = gather_stage(links, "x", yc.at[1], xregion(links))
    state = factor_some(9, 12, state)
    kt1, ht1 = kt, ht
    low, nt_, _ = factor_end(state)
    ss = small_back(links, ss, sz, sres)
    arrive(ps)
    ps = gather_stage(links, "k", yc.at[1], kregion(links))
    kr = make_k(unit_part(low, 2 * B), 1)
    yr = nn(low, aer[...]) - yrow
    nty = nn(nt_, yr)

    def image_free(lanes):
        yy[:, lanes] = nn(low, aec[:, lanes])
    chunks(image_free)
    arrive(fs)
    att = fres[0, :, 0:B] - nn(rows2, jnp.concatenate([kt1, ht1], axis=0))
    arrive(ps)
    arrive(ss)
    nd = coupling(low, nt_, att, sres[:, 128:128 + B], sres[:, 0:B])
    left = jnp.concatenate([nty + nn(nd, kr), kr], axis=0).T
    of_h = jnp.concatenate([nt_, nd], axis=1)

    def last(lanes):
        kcl = kc[:, lanes]
        hcl = nn(of_h, jnp.concatenate([yy[:, lanes] - yc[1, :, lanes], kcl], axis=0))
        o_ref[:, lanes] = o_ref[:, lanes] - nn(left, jnp.concatenate([kcl, hcl], axis=0))
    chunks(last)

    @pl.when(y == 0)
    def _():
        for j in range(1, NY):
            yscatter(j, lo, j).wait_send()
            yscatter(j, hi, NY + j).wait_send()

    @pl.when(row == 0)
    def _():
        for copy in core_copies:
            copy.wait_send()

    @pl.when(origin)
    def _():
        for j in range(1, NX):
            for g in range(3):
                xscatter(j, g).wait_send()

    @pl.when(z == 0)
    def _():
        for j in range(1, NZ):
            for g in range(3):
                zscatter(j, g).wait_send()

    links.finish()


def local(matrix):
    vmem = pltpu.VMEM

    def ysum_buffers(lead, n):
        return [vmem(lead + (n, B, 256), F32), vmem(lead + (NY, n, 24, 128), F32), vmem(lead + (n, B, 256), F32)]

    return pl.pallas_call(
        body,
        out_shape=jax.ShapeDtypeStruct((ROWS, COLS), F32),
        in_specs=[pl.BlockSpec(memory_space=pltpu.VMEM)],
        out_specs=pl.BlockSpec(memory_space=pltpu.VMEM),
        scratch_shapes=[
            vmem((3, B, ROWS), F32), vmem((3, B, ROWS), F32), vmem((3, B, COLS), F32),
            vmem((3, 48, COLS), F32), vmem((3, 48, 512), F32),
            vmem((2, B, COLS), F32), vmem((2, 48, COLS), F32), vmem((2, 48, COLS), F32),
            vmem((2, NX, 48, 512), F32), vmem((2, 48, 512), F32), vmem((2, NZ, 24, 128), F32), vmem((2, B, COLS), F32),
            *ysum_buffers((2,), 1), *ysum_buffers((2,), 1), *ysum_buffers((1,), 1), *ysum_buffers((), 2), *ysum_buffers((), 1),
            vmem((B, 256), F32), vmem((2, 24, 128), F32), vmem((NX, 24, 128), F32), vmem((NZ, 24, 128), F32), vmem((B, 256), F32),
            vmem((2, B, COLS), F32), vmem((2, B, ROWS), F32), vmem((B, COLS), F32), vmem((B, ROWS), F32),
            vmem((B, COLS), F32), vmem((B, COLS), F32), vmem((B, COLS), F32), vmem((B, 128), F32),
            pltpu.SemaphoreType.DMA((SEND_SEMS,)), pltpu.SemaphoreType.DMA((SEND_SEMS,)),
        ],
        compiler_params=pltpu.CompilerParams(
            collective_id=0, has_side_effects=True, vmem_limit_bytes=56 * 1024 * 1024),
        name="two_panels",
    )(matrix)


def solution(mesh):
    return jax.shard_map(local, mesh=mesh, in_specs=(P("row", "col"),), out_specs=P("row", "col"), check_vma=False)
```

```python
import jax
import jax.numpy as jnp
from jax import lax
from jax.experimental import pallas as pl
from jax.experimental.pallas import tpu as pltpu
from jax.sharding import PartitionSpec as P

B = 96
ROWS = 256
COLS = 2048
NX, NZ, NY = 4, 8, 8
F32 = jnp.float32
HIGH = lax.Precision.HIGHEST
MESH = pl.DeviceIdType.MESH

SEMS = 52
METER = 768


def nn(a, b):
    return lax.dot_general(a, b, (((1,), (0,)), ((), ())), precision=HIGH, preferred_element_type=F32)


def nt(a, b):
    return lax.dot_general(a, b, (((1,), (1,)), ((), ())), precision=HIGH, preferred_element_type=F32)


class Links:
    def __init__(self, send, recv, meter):
        self.send, self.recv, self.meter, self.count, self.open = send, recv, meter, 0, []
        row, self.y = lax.axis_index("row"), lax.axis_index("col")
        self.row = row
        self.x, self.z, self.k = row // 16, (row // 2) % 8, row % 2

    def sems(self, n):
        first = self.count
        self.count += n
        return first

    def at(self, kind, j):
        x, z, k, y = self.x, self.z, self.k, self.y
        if kind == "x":
            x = (x + j) % NX
        elif kind == "z":
            z = (z + j) % NZ
        elif kind == "k":
            k = (k + j) % 2
        else:
            y = (y + j) % NY
        return (x * 16 + z * 2 + k, y)

    def copy(self, src, dst, sem, kind, j):
        return pltpu.make_async_remote_copy(
            src_ref=src, dst_ref=dst, send_sem=self.send.at[sem], recv_sem=self.recv.at[sem],
            device_id=self.at(kind, j), device_id_type=MESH)

    def take(self, sem, words):
        whole = self.meter.at[pl.ds(0, words // 128), :]
        pltpu.make_async_copy(whole, whole, sem).wait()

    def finish(self):
        for sem, words in self.open:
            self.take(self.send.at[sem], words)


SIZE = {"x": NX, "z": NZ, "y": NY, "k": 2}


def words_of(ref):
    n = 1
    for size in ref.shape:
        n *= size
    return n


def exchange(links, kind, src_of, dst_of):
    sem = links.sems(1)
    words = 0
    for j in range(1, SIZE[kind]):
        src = src_of(j)
        words += words_of(src)
        links.copy(src, dst_of(j), sem, kind, j).start()
    links.open.append((sem, words))
    return links, sem, words


def arrive(coming):
    links, sem, words = coming
    links.take(links.recv.at[sem], words)


def place(links, kind, j):
    return (getattr(links, kind) + j) % SIZE[kind]


def ypiece(j):
    return pl.ds(pl.multiple_of(24 * (j // 2), 8), 24), pl.ds(pl.multiple_of(128 * (j % 2), 128), 128)


def zpiece(j):
    return ypiece_rows(j), pl.ds(pl.multiple_of(128 * (j // 2), 128), 128)


def ypiece_rows(j):
    return pl.ds(pl.multiple_of(24 * (j % 2), 8), 24)


def zregion(links):
    return (pl.ds(pl.multiple_of(48 * links.k + 24 * (links.z % 2), 8), 24),
            pl.ds(pl.multiple_of(512 * links.x + 128 * (links.z // 2), 128), 128))


def xregion(links):
    return (pl.ds(pl.multiple_of(48 * links.k, 8), 48),
            pl.ds(pl.multiple_of(512 * links.x, 128), 512))


def kregion(links):
    return pl.ds(pl.multiple_of(48 * links.k, 8), 48), slice(None)


def gather_stage(links, kind, ref, region):
    view = ref.at[region]
    return exchange(links, kind, lambda j: view, lambda j: view)


def ysum_start(links, src, buf):
    return exchange(links, "y",
                    lambda j: src.at[(slice(None),) + ypiece(place(links, "y", j))],
                    lambda j: buf.at[j])


def ysum_mid(links, copies, src, buf, res):
    mine = (slice(None),) + ypiece(links.y)
    arrive(copies)
    total = src[mine]
    for j in range(1, NY):
        total = total + buf[j]
    res[mine] = total
    return gather_stage(links, "y", res, mine)


def psum_core(links, part, bufk):
    rows = pl.ds(pl.multiple_of(48 * (1 - links.k), 8), 48)
    return exchange(links, "k", lambda j: part.at[rows, :], lambda j: bufk)


def psum_x(links, copies, part, bufk, sumk, bufx):
    arrive(copies)
    rows = pl.ds(pl.multiple_of(48 * links.k, 8), 48)
    sumk[...] = part[rows, :] + bufk[...]
    return exchange(links, "x",
                    lambda j: sumk.at[:, pl.ds(pl.multiple_of(512 * place(links, "x", j), 128), 512)],
                    lambda j: bufx.at[j])


def psum_z(links, copies, sumk, bufx, sumx, bufz):
    arrive(copies)
    total = sumk[:, pl.ds(pl.multiple_of(512 * links.x, 128), 512)]
    for j in range(1, NX):
        total = total + bufx[j]
    sumx[...] = total
    return exchange(links, "z", lambda j: sumx.at[zpiece(place(links, "z", j))], lambda j: bufz.at[j])


def psum_back_z(links, copies, sumx, bufz, out):
    arrive(copies)
    total = sumx[zpiece(links.z)]
    for j in range(1, NZ):
        total = total + bufz[j]
    region = zregion(links)
    out[region] = total
    return gather_stage(links, "z", out, region)


def small_core(links, src, parts):
    parts[links.k] = src[ypiece(links.y)]
    view = parts.at[links.k]
    return exchange(links, "k", lambda j: view, lambda j: view)


def small_next(links, copies, kind, before, parts):
    arrive(copies)
    total = before[0]
    for j in range(1, before.shape[0]):
        total = total + before[j]
    here = getattr(links, kind)
    parts[here] = total
    view = parts.at[here]
    return exchange(links, kind, lambda j: view, lambda j: view)


def small_back(links, copies, zparts, out):
    arrive(copies)
    total = zparts[0]
    for j in range(1, NZ):
        total = total + zparts[j]
    mine = ypiece(links.y)
    out[mine] = total
    return gather_stage(links, "y", out, mine)


def factor_block(b, carry):
    w, v, e, low = carry
    row = lax.broadcasted_iota(jnp.int32, (B, 128), 0)
    lane = lax.broadcasted_iota(jnp.int32, (B, 128), 1)
    lane1 = lane[0:1]
    alive = row < B - 8 * b
    for first in range(0, 8, 4):
        steps = range(first, first + 4)
        wcol = [jnp.broadcast_to(w[:, s:s + 1], (B, 128)) for s in steps]
        vcol = [jnp.broadcast_to(v[:, s:s + 1], (B, 128)) for s in steps]
        wrow = [w[s:s + 1, :] for s in steps]
        vrow = [v[s:s + 1, :] for s in steps]
        erow = [e[s:s + 1, :] for s in steps]
        for i, s in enumerate(steps):
            rs = lax.rsqrt(wcol[i][s:s + 1, :])
            col = jnp.where(alive & (row >= s), wcol[i] * rs, 0.0)
            wr = wrow[i] * rs
            er = erow[i] * rs
            vc = vcol[i] + col
            ip = 1.0 / vc[s:s + 1, :]
            vr = jnp.where(lane1 == s, -1.0, vrow[i]) * ip
            vm = jnp.where(row == s, 1.0, vc)
            for j in range(i + 1, 4):
                t = first + j
                cj = col[t:t + 1, :]
                wcol[j] = wcol[j] - col * cj
                wrow[j] = wrow[j] - cj * wr
                erow[j] = erow[j] - cj * er
                vj = vcol[j][s:s + 1, :] * ip
                vcol[j] = jnp.where(row == s, 0.0, vcol[j]) - vm * vj
                vrow[j] = jnp.where(lane1 == s, 0.0, vrow[j]) - vm[t:t + 1, :] * vr
            w = w - col * wr
            low = jnp.where(lane == s, col, low)
            e = jnp.where(row == s, jnp.broadcast_to(er, (B, 128)), e - jnp.where(row > s, col, 0.0) * er)
            v = jnp.where((lane == s) | (row == s), 0.0, v) - vm * vr

    def turn(m):
        m = pltpu.roll(m, 120, axis=1)
        return jnp.concatenate([m[8:], m[:8]], axis=0)

    e = jnp.concatenate([e[8:], e[:8]], axis=0)
    return turn(w), turn(v), e, turn(low)


def factor_start(gram, top):
    row = lax.broadcasted_iota(jnp.int32, (B, 128), 0)
    lane = lax.broadcasted_iota(jnp.int32, (B, 128), 1)
    return gram, -top, (row == lane).astype(F32), jnp.zeros((B, 128), F32)


def factor_some(first, last, state):
    return lax.fori_loop(first, last, factor_block, state)


def factor_end(state):
    _, v, e, low = state
    low = pltpu.roll(low, 96, axis=1)[:, 0:B]
    v = pltpu.roll(v, 96, axis=1)
    return low, nn(v.T[0:B], e)[:, 0:B], e[:, 0:B]


def body(a_ref, o_ref, wsrc, wr, wc, stgk, stgx,
         part, bufk, sumk, bufx, sumx, bufz, yc,
         gsrc, gbuf, gres, rsrc, rbuf, rres, csrc, cbuf, cres, esrc, ebuf, eres, fsrc, fbuf, fres,
         ssrc, sk, sx, sz, sres,
         pcs, prs, aec, aer, yy, kc, hc, sq, meter, send, recv):
    links = Links(send, recv, meter)
    x, z, k, y, row = links.x, links.z, links.k, links.y, links.row

    barrier = pltpu.get_barrier_semaphore()
    for kind in ("y", "x", "z", "k"):
        for j in range(1, SIZE[kind]):
            pl.semaphore_signal(barrier, inc=1, device_id=links.at(kind, j), device_id_type=MESH)

    @pl.when(y == 0)
    def _():
        wsrc[0] = a_ref[:, 0:128].T[0:B]

    pl.semaphore_wait(barrier, NY - 1 + NX - 1 + NZ - 1 + 1)

    lo, hi = (pl.ds(0, 1), pl.ds(1, 2))
    origin = (x == 0) & (z == 0)

    ysc = links.sems(2)
    core = links.sems(3)
    xsc = links.sems(3)
    zsc = links.sems(3)
    mine = ypiece(y)

    def yscatter(j, part_, g):
        piece = (part_,) + ypiece(j)
        return links.copy(wsrc.at[piece], wr.at[piece], ysc + g, "y", j)

    core_copies = [links.copy(a_ref.at[pl.ds(48, 48), :], stgk.at[0], core, "k", 1),
                   links.copy(a_ref.at[pl.ds(144, 48), :], stgk.at[1], core + 1, "k", 1),
                   links.copy(a_ref.at[pl.ds(240, 16), :], stgk.at[2, pl.ds(0, 16), :], core + 2, "k", 1)]

    def xscatter(j, g):
        return links.copy(stgk.at[g, :, pl.ds(512 * j, 512)], stgx.at[g], xsc + g, "x", j)

    def zscatter(j, g):
        rows, lanes = zpiece(j)
        to_rows = pl.ds(pl.multiple_of(48 * k + 24 * (j % 2), 8), 24)
        to_lanes = pl.ds(pl.multiple_of(512 * x + 128 * (j // 2), 128), 128)
        return links.copy(stgx.at[g, rows, lanes], wc.at[g, to_rows, to_lanes], zsc + g, "z", j)

    def y_out(part_, g):
        @pl.when(y == 0)
        def _():
            wr[(part_,) + ypiece(0)] = wsrc[(part_,) + ypiece(0)]
            for j in range(1, NY):
                yscatter(j, part_, g).start()

    def y_in(part_, g):
        piece = (part_,) + mine

        @pl.when(y != 0)
        def _():
            links.copy(wr.at[piece], wr.at[piece], ysc + g, "y", 0).wait_recv()

        return gather_stage(links, "y", wr, piece)

    def x_out(g):
        @pl.when(origin)
        def _():
            @pl.when(k == 1)
            def _():
                core_copies[g].wait_recv()
            for j in range(1, NX):
                xscatter(j, g).start()
            stgx[g] = stgk[g, :, 0:512]

    def z_out(g):
        @pl.when(z == 0)
        def _():
            @pl.when(x != 0)
            def _():
                links.copy(stgx.at[g], stgx.at[g], xsc + g, "x", 0).wait_recv()
            for j in range(1, NZ):
                zscatter(j, g).start()
            wc[(g,) + zregion(links)] = stgx[(g,) + zpiece(0)]

    def z_in(g):
        region = (g,) + zregion(links)

        @pl.when(z != 0)
        def _():
            links.copy(wc.at[region], wc.at[region], zsc + g, "z", 0).wait_recv()

        return gather_stage(links, "z", wc, region)

    y_out(lo, 0)

    @pl.when(row == 0)
    def _():
        core_copies[0].start()
        stgk[0] = a_ref[0:48, :]
        for copy in core_copies[1:]:
            copy.start()

    x_out(0)

    @pl.when(row == 0)
    def _():
        stgk[1] = a_ref[96:144, :]
        stgk[2] = a_ref[192:240, :]

    @pl.when(row == 1)
    def _():
        stgk[2, 16:48, :] = a_ref[0:32, :]

    wr_lo = y_in(lo, 0)
    z_out(0)

    gl_r = row * ROWS + lax.broadcasted_iota(jnp.int32, (B, ROWS), 1)
    gl_c = y * COLS + lax.broadcasted_iota(jnp.int32, (B, COLS), 1)
    lane128 = lax.broadcasted_iota(jnp.int32, (B, 128), 1)
    first_col = y == 0

    def chunks(step):
        def run(i, _):
            step(pl.ds(pl.multiple_of(512 * i, 512), 512))
            return 0
        lax.fori_loop(0, 4, run, 0)

    def product_cols(pr, mat, out):
        def step(lanes):
            out[:, lanes] = nn(pr, mat[:, lanes])
        chunks(step)

    def product_rows(pc, mat, width):
        def step(i, acc):
            lanes = pl.ds(pl.multiple_of(512 * i, 512), 512)
            return acc + nt(pc[:, lanes], mat[:, lanes])
        return lax.fori_loop(0, 4, step, jnp.zeros((B, width), F32))

    def widen(m):
        sq[...] = jnp.zeros((B, 128), F32)
        sq[:, 0:B] = m
        return sq[...]

    def square(window, at):
        width = window.shape[1]
        return jnp.where(lane128 < B, pltpu.roll(window, width - at, axis=1)[:, 0:128], 0.0)

    def col_square(ref, at):
        return jnp.where(first_col, square(ref[:, 0:384], at), 0.0)

    def unit_part(chol, trail):
        wide = jnp.concatenate([widen(chol), jnp.zeros((B, 384), F32)], axis=1)
        return pltpu.roll(wide, trail, axis=1)

    def make_k(unit, p):
        kc[...] = -pcs[p]
        kc[:, 0:512] = kc[:, 0:512] + jnp.where(first_col, unit, 0.0)
        return (jnp.where(row == 0, unit[:, 0:256], 0.0) + jnp.where(row == 1, unit[:, 256:512], 0.0)) - prs[p]

    arrive(wr_lo)
    prs[0] = jnp.where(gl_r >= B, wr[0], 0.0)
    product_cols(prs[0], a_ref, part.at[0])
    ps = psum_core(links, part.at[0], bufk.at[0])

    @pl.when(y == 0)
    def _():
        t = a_ref[:, 0:384].T
        wsrc[1] = t[B:2 * B]
        wsrc[2] = t[2 * B:3 * B]

    y_out(hi, 1)
    w0 = z_in(0)
    ps = psum_x(links, ps, part.at[0], bufk.at[0], sumk.at[0], bufx.at[0])
    arrive(w0)
    w0 = gather_stage(links, "x", wc, (0,) + xregion(links))
    ps = psum_z(links, ps, sumk.at[0], bufx.at[0], sumx.at[0], bufz.at[0])
    x_out(1)
    wr_hi = y_in(hi, 1)
    arrive(w0)
    w0 = gather_stage(links, "k", wc, (0,) + kregion(links))
    ps = psum_back_z(links, ps, sumx.at[0], bufz.at[0], yc.at[0])
    z_out(1)
    arrive(w0)
    pcs[0] = jnp.where(gl_c >= B, wc[0], 0.0)
    gsrc[0, 0, :, 0:128] = widen(product_rows(pcs.at[0], pcs.at[0], B))
    gsrc[0, 0, :, 128:256] = col_square(pcs.at[0], B)
    gs = ysum_start(links, gsrc.at[0], gbuf.at[0])
    rsrc[0, 0] = product_rows(pcs.at[0], a_ref, ROWS)
    arrive(ps)
    ps = gather_stage(links, "x", yc.at[0], xregion(links))
    w1 = z_in(1)
    gs = ysum_mid(links, gs, gsrc.at[0], gbuf.at[0], gres.at[0])
    rs = ysum_start(links, rsrc.at[0], rbuf.at[0])
    x_out(2)
    arrive(ps)
    ps = gather_stage(links, "k", yc.at[0], kregion(links))
    arrive(w1)
    w1 = gather_stage(links, "x", wc, (1,) + xregion(links))
    arrive(ps)
    csrc[0, 0, :, 0:128] = widen(product_rows(pcs.at[0], yc.at[0], B))
    csrc[0, 0, :, 128:256] = col_square(yc.at[0], B)
    cs = ysum_start(links, csrc.at[0], cbuf.at[0])
    rs = ysum_mid(links, rs, rsrc.at[0], rbuf.at[0], rres.at[0])
    z_out(2)
    arrive(gs)
    top = gres[0, 0, :, 128:256]
    state = factor_some(0, 6, factor_start(gres[0, 0, :, 0:128], top))
    arrive(w1)
    w1 = gather_stage(links, "k", wc, (1,) + kregion(links))
    state = factor_some(6, 8, state)
    arrive(w1)
    esrc[0, :, 0:128] = col_square(wc.at[1], B)
    esrc[0, :, 128:256] = col_square(yc.at[0], 2 * B)
    esrc[1, :, 0:128] = col_square(wc.at[0], 2 * B)
    esrc[1, :, 128:256] = col_square(wc.at[1], 2 * B)
    es = ysum_start(links, esrc, ebuf)
    cs = ysum_mid(links, cs, csrc.at[0], cbuf.at[0], cres.at[0])
    state = factor_some(8, 12, state)
    low, nt_, inv = factor_end(state)
    unit = unit_part(low, B)
    kr = make_k(unit, 0)

    def image(lanes):
        yy[:, lanes] = nn(low, wc[1, :, lanes]) - yc[0, :, lanes]
    chunks(image)
    es = ysum_mid(links, es, esrc, ebuf, eres)
    w2 = z_in(2)
    arrive(rs)
    arrive(wr_hi)
    yrow = rres[0, 0]
    yr = nn(low, wr[1]) - yrow
    arrive(cs)

    yt, phi = cres[0, 0, :, 128:128 + B], cres[0, 0, :, 0:B]
    of_k = -nn(inv, nt(nt(yt, low) - phi, nt_))
    of_both = jnp.concatenate([inv, of_k], axis=1)

    def next_panel(lanes):
        pcs[1, :, lanes] = nn(of_both, jnp.concatenate([yc[0, :, lanes], kc[:, lanes]], axis=0))
    chunks(next_panel)
    pcs[1] = jnp.where(gl_c >= 2 * B, pcs[1], 0.0)
    gsrc[1, 0, :, 0:128] = widen(product_rows(pcs.at[1], pcs.at[1], B))
    gsrc[1, 0, :, 128:256] = col_square(pcs.at[1], 2 * B)
    gs = ysum_start(links, gsrc.at[1], gbuf.at[1])
    prs[1] = jnp.where(gl_r >= 2 * B, nn(of_both, jnp.concatenate([yrow, kr], axis=0)), 0.0)
    arrive(w2)
    w2 = gather_stage(links, "x", wc, (2,) + xregion(links))

    def coupling(low, nt_, att, yt, phi):
        c = nt(nn(low, att) - yt, low) - nt(low, yt) + phi
        return -0.5 * nt(nn(nt_, c), nt_)

    arrive(es)
    nd = coupling(low, nt_, eres[0, :, 0:B], yt, phi)
    hr = nn(nt_, yr) + nn(nd, kr)
    right_r = jnp.concatenate([kr, hr], axis=0)
    left = jnp.concatenate([hr, kr], axis=0).T
    of_h = jnp.concatenate([nt_, nd], axis=1)

    prow = prs[1]

    def update(i, acc):
        lanes = pl.ds(pl.multiple_of(512 * i, 512), 512)
        kcl = kc[:, lanes]
        hcl = nn(of_h, jnp.concatenate([yy[:, lanes], kcl], axis=0))
        hc[:, lanes] = hcl
        fresh = a_ref[:, lanes] - nn(left, jnp.concatenate([kcl, hcl], axis=0))
        o_ref[:, lanes] = fresh
        part[1, :, lanes] = nn(prow, fresh)
        return acc + nt(pcs[1, :, lanes], fresh)
    rsrc[1, 0] = lax.fori_loop(0, 4, update, jnp.zeros((B, ROWS), F32))
    rs = ysum_start(links, rsrc.at[1], rbuf.at[1])
    ps = psum_core(links, part.at[1], bufk.at[1])
    gs = ysum_mid(links, gs, gsrc.at[1], gbuf.at[1], gres.at[1])
    arrive(w2)
    w2 = gather_stage(links, "k", wc, (2,) + kregion(links))
    ps = psum_x(links, ps, part.at[1], bufk.at[1], sumk.at[1], bufx.at[1])
    kt = -eres[1, :, 0:B]
    ht = nn(nt_, nn(low, eres[1, :, 128:128 + B]) - eres[0, :, 128:128 + B]) + nn(nd, kt)
    rows2 = jnp.concatenate([ht, kt], axis=0).T
    aer[...] = wr[2] - nn(rows2, right_r)
    arrive(w2)
    fsrc[0, :, 0:128] = col_square(wc.at[2], 2 * B)
    fsrc[0, :, 128:256] = jnp.zeros((B, 128), F32)
    fs = ysum_start(links, fsrc, fbuf)

    def next_rows(lanes):
        aec[:, lanes] = wc[2, :, lanes] - nn(rows2, jnp.concatenate([kc[:, lanes], hc[:, lanes]], axis=0))
    chunks(next_rows)
    rs = ysum_mid(links, rs, rsrc.at[1], rbuf.at[1], rres.at[1])
    ps = psum_z(links, ps, sumk.at[1], bufx.at[1], sumx.at[1], bufz.at[1])
    arrive(gs)
    top = gres[1, 0, :, 128:256]
    state = factor_some(0, 5, factor_start(gres[1, 0, :, 0:128], top))
    arrive(rs)
    yrow = rres[1, 0]
    none = jnp.zeros((B, ROWS), F32)
    ssrc[:, 0:128] = widen(nt(prs[1], yrow))
    ssrc[:, 128:256] = (jnp.where(row == 0, square(jnp.concatenate([yrow, none], axis=1), 2 * B), 0.0)
                        + jnp.where(row == 1, square(jnp.concatenate([none, yrow], axis=1), 2 * B), 0.0))
    ss = small_core(links, ssrc, sk)
    fs = ysum_mid(links, fs, fsrc, fbuf, fres)
    ps = psum_back_z(links, ps, sumx.at[1], bufz.at[1], yc.at[1])
    ss = small_next(links, ss, "x", sk, sx)
    state = factor_some(5, 9, state)
    ss = small_next(links, ss, "z", sx, sz)
    arrive(ps)
    ps = gather_stage(links, "x", yc.at[1], xregion(links))
    state = factor_some(9, 12, state)
    kt1, ht1 = kt, ht
    low, nt_, _ = factor_end(state)
    ss = small_back(links, ss, sz, sres)
    arrive(ps)
    ps = gather_stage(links, "k", yc.at[1], kregion(links))
    kr = make_k(unit_part(low, 2 * B), 1)
    yr = nn(low, aer[...]) - yrow
    nty = nn(nt_, yr)

    def image_free(lanes):
        yy[:, lanes] = nn(low, aec[:, lanes])
    chunks(image_free)
    arrive(fs)
    att = fres[0, :, 0:B] - nn(rows2, jnp.concatenate([kt1, ht1], axis=0))
    arrive(ps)
    arrive(ss)
    nd = coupling(low, nt_, att, sres[:, 128:128 + B], sres[:, 0:B])
    left = jnp.concatenate([nty + nn(nd, kr), kr], axis=0).T
    of_h = jnp.concatenate([nt_, nd], axis=1)

    def last(lanes):
        kcl = kc[:, lanes]
        hcl = nn(of_h, jnp.concatenate([yy[:, lanes] - yc[1, :, lanes], kcl], axis=0))
        o_ref[:, lanes] = o_ref[:, lanes] - nn(left, jnp.concatenate([kcl, hcl], axis=0))
    chunks(last)

    @pl.when(y == 0)
    def _():
        for g, panels in ((0, 1), (1, 2)):
            links.take(send.at[ysc + g], (NY - 1) * panels * 24 * 128)

    @pl.when(row == 0)
    def _():
        for copy in core_copies:
            copy.wait_send()

    @pl.when(origin)
    def _():
        for g in range(3):
            links.take(send.at[xsc + g], (NX - 1) * 48 * 512)

    @pl.when(z == 0)
    def _():
        for g in range(3):
            links.take(send.at[zsc + g], (NZ - 1) * 24 * 128)

    links.finish()


def local(matrix):
    vmem = pltpu.VMEM

    def ysum_buffers(lead, n):
        return [vmem(lead + (n, B, 256), F32), vmem(lead + (NY, n, 24, 128), F32), vmem(lead + (n, B, 256), F32)]

    return pl.pallas_call(
        body,
        out_shape=jax.ShapeDtypeStruct((ROWS, COLS), F32),
        in_specs=[pl.BlockSpec(memory_space=pltpu.VMEM)],
        out_specs=pl.BlockSpec(memory_space=pltpu.VMEM),
        scratch_shapes=[
            vmem((3, B, ROWS), F32), vmem((3, B, ROWS), F32), vmem((3, B, COLS), F32),
            vmem((3, 48, COLS), F32), vmem((3, 48, 512), F32),
            vmem((2, B, COLS), F32), vmem((2, 48, COLS), F32), vmem((2, 48, COLS), F32),
            vmem((2, NX, 48, 512), F32), vmem((2, 48, 512), F32), vmem((2, NZ, 24, 128), F32), vmem((2, B, COLS), F32),
            *ysum_buffers((2,), 1), *ysum_buffers((2,), 1), *ysum_buffers((1,), 1), *ysum_buffers((), 2), *ysum_buffers((), 1),
            vmem((B, 256), F32), vmem((2, 24, 128), F32), vmem((NX, 24, 128), F32), vmem((NZ, 24, 128), F32), vmem((B, 256), F32),
            vmem((2, B, COLS), F32), vmem((2, B, ROWS), F32), vmem((B, COLS), F32), vmem((B, ROWS), F32),
            vmem((B, COLS), F32), vmem((B, COLS), F32), vmem((B, COLS), F32), vmem((B, 128), F32),
            vmem((METER, 128), F32),
            pltpu.SemaphoreType.DMA((SEMS,)), pltpu.SemaphoreType.DMA((SEMS,)),
        ],
        compiler_params=pltpu.CompilerParams(
            collective_id=0, has_side_effects=True, vmem_limit_bytes=56 * 1024 * 1024),
        name="two_panels",
    )(matrix)


def solution(mesh):
    return jax.shard_map(local, mesh=mesh, in_specs=(P("row", "col"),), out_specs=P("row", "col"), check_vma=False)
```

```python
import jax
import jax.numpy as jnp
from jax import lax
from jax.experimental import pallas as pl
from jax.experimental.pallas import tpu as pltpu
from jax.sharding import PartitionSpec as P

B = 96
ROWS = 256
COLS = 2048
NX, NZ, NY = 4, 8, 8
F32 = jnp.float32
HIGH = lax.Precision.HIGHEST
MESH = pl.DeviceIdType.MESH

SEMS = 53
METER = 1344


def nn(a, b):
    return lax.dot_general(a, b, (((1,), (0,)), ((), ())), precision=HIGH, preferred_element_type=F32)


def nt(a, b):
    return lax.dot_general(a, b, (((1,), (1,)), ((), ())), precision=HIGH, preferred_element_type=F32)


class Links:
    def __init__(self, send, recv, meter):
        self.send, self.recv, self.meter, self.count, self.open = send, recv, meter, 0, []
        row, self.y = lax.axis_index("row"), lax.axis_index("col")
        self.row = row
        self.x, self.z, self.k = row // 16, (row // 2) % 8, row % 2

    def sems(self, n):
        first = self.count
        self.count += n
        return first

    def at(self, kind, j):
        x, z, k, y = self.x, self.z, self.k, self.y
        if kind == "x":
            x = (x + j) % NX
        elif kind == "z":
            z = (z + j) % NZ
        elif kind == "k":
            k = (k + j) % 2
        else:
            y = (y + j) % NY
        return (x * 16 + z * 2 + k, y)

    def copy(self, src, dst, sem, kind, j):
        return pltpu.make_async_remote_copy(
            src_ref=src, dst_ref=dst, send_sem=self.send.at[sem], recv_sem=self.recv.at[sem],
            device_id=self.at(kind, j), device_id_type=MESH)

    def take(self, sem, words):
        whole = self.meter.at[pl.ds(0, words // 128), :]
        pltpu.make_async_copy(whole, whole, sem).wait()

    def finish(self):
        for sem, words in self.open:
            self.take(self.send.at[sem], words)


SIZE = {"x": NX, "z": NZ, "y": NY, "k": 2}


def words_of(ref):
    n = 1
    for size in ref.shape:
        n *= size
    return n


def exchange(links, kind, src_of, dst_of):
    sem = links.sems(1)
    words = 0
    for j in range(1, SIZE[kind]):
        src = src_of(j)
        words += words_of(src)
        links.copy(src, dst_of(j), sem, kind, j).start()
    links.open.append((sem, words))
    return links, sem, words


def arrive(coming):
    links, sem, words = coming
    links.take(links.recv.at[sem], words)


def place(links, kind, j):
    return (getattr(links, kind) + j) % SIZE[kind]


def ypiece(j):
    return pl.ds(pl.multiple_of(24 * (j // 2), 8), 24), pl.ds(pl.multiple_of(128 * (j % 2), 128), 128)


def zpiece(j):
    return ypiece_rows(j), pl.ds(pl.multiple_of(128 * (j // 2), 128), 128)


def ypiece_rows(j):
    return pl.ds(pl.multiple_of(24 * (j % 2), 8), 24)


def zregion(links):
    return (pl.ds(pl.multiple_of(48 * links.k + 24 * (links.z % 2), 8), 24),
            pl.ds(pl.multiple_of(512 * links.x + 128 * (links.z // 2), 128), 128))


def xregion(links):
    return (pl.ds(pl.multiple_of(48 * links.k, 8), 48),
            pl.ds(pl.multiple_of(512 * links.x, 128), 512))


def kregion(links):
    return pl.ds(pl.multiple_of(48 * links.k, 8), 48), slice(None)


def gather_stage(links, kind, ref, region):
    view = ref.at[region]
    return exchange(links, kind, lambda j: view, lambda j: view)


def ysum_start(links, src, buf):
    return exchange(links, "y",
                    lambda j: src.at[(slice(None),) + ypiece(place(links, "y", j))],
                    lambda j: buf.at[j])


def ysum_mid(links, copies, src, buf, res):
    mine = (slice(None),) + ypiece(links.y)
    arrive(copies)
    total = src[mine]
    for j in range(1, NY):
        total = total + buf[j]
    res[mine] = total
    return gather_stage(links, "y", res, mine)


def half_start(links, src, parts, head, sem):
    rows = pl.ds(pl.multiple_of(48 * links.k, 8), 48)
    parts[links.y] = src[rows, 0:128]
    view = parts.at[links.y]
    coming = exchange(links, "y", lambda j: view, lambda j: view)

    @pl.when(links.y == 0)
    def _():
        head[...] = src[rows, 128:256]
        for j in range(1, NY):
            links.copy(head, head, sem, "y", j).start()

    return coming


def half_mid(links, coming, parts, head, sem, res):
    rows = pl.ds(pl.multiple_of(48 * links.k, 8), 48)
    arrive(coming)

    @pl.when(links.y != 0)
    def _():
        links.copy(head, head, sem, "y", 0).wait_recv()

    total = parts[0]
    for j in range(1, NY):
        total = total + parts[j]
    res[rows, 0:128] = total
    res[rows, 128:256] = head[...]
    return gather_stage(links, "k", res, kregion(links))


def psum_core(links, part, bufk):
    rows = pl.ds(pl.multiple_of(48 * (1 - links.k), 8), 48)
    return exchange(links, "k", lambda j: part.at[rows, :], lambda j: bufk)


def psum_x(links, copies, part, bufk, sumk, bufx):
    arrive(copies)
    rows = pl.ds(pl.multiple_of(48 * links.k, 8), 48)
    sumk[...] = part[rows, :] + bufk[...]
    return exchange(links, "x",
                    lambda j: sumk.at[:, pl.ds(pl.multiple_of(512 * place(links, "x", j), 128), 512)],
                    lambda j: bufx.at[j])


def psum_z(links, copies, sumk, bufx, sumx, bufz):
    arrive(copies)
    total = sumk[:, pl.ds(pl.multiple_of(512 * links.x, 128), 512)]
    for j in range(1, NX):
        total = total + bufx[j]
    sumx[...] = total
    return exchange(links, "z", lambda j: sumx.at[zpiece(place(links, "z", j))], lambda j: bufz.at[j])


def psum_back_z(links, copies, sumx, bufz, out):
    arrive(copies)
    total = sumx[zpiece(links.z)]
    for j in range(1, NZ):
        total = total + bufz[j]
    region = zregion(links)
    out[region] = total
    return gather_stage(links, "z", out, region)


def small_core(links, src, parts):
    parts[links.k] = src[ypiece(links.y)]
    view = parts.at[links.k]
    return exchange(links, "k", lambda j: view, lambda j: view)


def small_next(links, copies, kind, before, parts):
    arrive(copies)
    total = before[0]
    for j in range(1, before.shape[0]):
        total = total + before[j]
    here = getattr(links, kind)
    parts[here] = total
    view = parts.at[here]
    return exchange(links, kind, lambda j: view, lambda j: view)


def small_back(links, copies, zparts, out):
    arrive(copies)
    total = zparts[0]
    for j in range(1, NZ):
        total = total + zparts[j]
    mine = ypiece(links.y)
    out[mine] = total
    return gather_stage(links, "y", out, mine)


def factor_block(b, carry):
    w, v, e, low = carry
    row = lax.broadcasted_iota(jnp.int32, (B, 128), 0)
    lane = lax.broadcasted_iota(jnp.int32, (B, 128), 1)
    lane1 = lane[0:1]
    alive = row < B - 8 * b
    for first in range(0, 8, 4):
        steps = range(first, first + 4)
        wcol = [jnp.broadcast_to(w[:, s:s + 1], (B, 128)) for s in steps]
        vcol = [jnp.broadcast_to(v[:, s:s + 1], (B, 128)) for s in steps]
        wrow = [w[s:s + 1, :] for s in steps]
        vrow = [v[s:s + 1, :] for s in steps]
        erow = [e[s:s + 1, :] for s in steps]
        for i, s in enumerate(steps):
            rs = lax.rsqrt(wcol[i][s:s + 1, :])
            col = jnp.where(alive & (row >= s), wcol[i] * rs, 0.0)
            wr = wrow[i] * rs
            er = erow[i] * rs
            vc = vcol[i] + col
            ip = 1.0 / vc[s:s + 1, :]
            vr = jnp.where(lane1 == s, -1.0, vrow[i]) * ip
            vm = jnp.where(row == s, 1.0, vc)
            for j in range(i + 1, 4):
                t = first + j
                cj = col[t:t + 1, :]
                wcol[j] = wcol[j] - col * cj
                wrow[j] = wrow[j] - cj * wr
                erow[j] = erow[j] - cj * er
                vj = vcol[j][s:s + 1, :] * ip
                vcol[j] = jnp.where(row == s, 0.0, vcol[j]) - vm * vj
                vrow[j] = jnp.where(lane1 == s, 0.0, vrow[j]) - vm[t:t + 1, :] * vr
            w = w - col * wr
            low = jnp.where(lane == s, col, low)
            e = jnp.where(row == s, jnp.broadcast_to(er, (B, 128)), e - jnp.where(row > s, col, 0.0) * er)
            v = jnp.where((lane == s) | (row == s), 0.0, v) - vm * vr

    def turn(m):
        m = pltpu.roll(m, 120, axis=1)
        return jnp.concatenate([m[8:], m[:8]], axis=0)

    e = jnp.concatenate([e[8:], e[:8]], axis=0)
    return turn(w), turn(v), e, turn(low)


def factor_start(gram, top):
    row = lax.broadcasted_iota(jnp.int32, (B, 128), 0)
    lane = lax.broadcasted_iota(jnp.int32, (B, 128), 1)
    return gram, -top, (row == lane).astype(F32), jnp.zeros((B, 128), F32)


def factor_some(first, last, state):
    return lax.fori_loop(first, last, factor_block, state)


def factor_end(state):
    _, v, e, low = state
    low = pltpu.roll(low, 96, axis=1)[:, 0:B]
    v = pltpu.roll(v, 96, axis=1)
    return low, nn(v.T[0:B], e)[:, 0:B], e[:, 0:B]


def body(a_ref, o_ref, wsrc, wr, wc, stgk, stgx,
         part, bufk, sumk, bufx, sumx, bufz, yc,
         gsrc, gbuf, gres, rsrc, rbuf, rres, csrc, cparts, chead, cres, gparts, ghead, esrc, ebuf, eres, fsrc, fbuf, fres,
         ssrc, sk, sx, sz, sres,
         pcs, prs, aec, aer, im, yy, kc, hc, sq, meter, send, recv):
    links = Links(send, recv, meter)
    x, z, k, y, row = links.x, links.z, links.k, links.y, links.row

    barrier = pltpu.get_barrier_semaphore()
    for kind in ("y", "x", "z", "k"):
        for j in range(1, SIZE[kind]):
            pl.semaphore_signal(barrier, inc=1, device_id=links.at(kind, j), device_id_type=MESH)

    @pl.when(y == 0)
    def _():
        wsrc[0] = a_ref[:, 0:128].T[0:B]

    pl.semaphore_wait(barrier, NY - 1 + NX - 1 + NZ - 1 + 1)

    lo, hi = (pl.ds(0, 1), pl.ds(1, 2))
    origin = (x == 0) & (z == 0)

    ysc = links.sems(2)
    hsem = links.sems(2)
    core = links.sems(3)
    xsc = links.sems(3)
    zsc = links.sems(3)
    mine = ypiece(y)

    def yscatter(j, part_, g):
        piece = (part_,) + ypiece(j)
        return links.copy(wsrc.at[piece], wr.at[piece], ysc + g, "y", j)

    core_copies = [links.copy(a_ref.at[pl.ds(48, 48), :], stgk.at[0], core, "k", 1),
                   links.copy(a_ref.at[pl.ds(144, 48), :], stgk.at[1], core + 1, "k", 1),
                   links.copy(a_ref.at[pl.ds(240, 16), :], stgk.at[2, pl.ds(0, 16), :], core + 2, "k", 1)]

    def xscatter(j, g):
        return links.copy(stgk.at[g, :, pl.ds(512 * j, 512)], stgx.at[g], xsc + g, "x", j)

    def zscatter(j, g):
        rows, lanes = zpiece(j)
        to_rows = pl.ds(pl.multiple_of(48 * k + 24 * (j % 2), 8), 24)
        to_lanes = pl.ds(pl.multiple_of(512 * x + 128 * (j // 2), 128), 128)
        return links.copy(stgx.at[g, rows, lanes], wc.at[g, to_rows, to_lanes], zsc + g, "z", j)

    def y_out(part_, g):
        @pl.when(y == 0)
        def _():
            wr[(part_,) + ypiece(0)] = wsrc[(part_,) + ypiece(0)]
            for j in range(1, NY):
                yscatter(j, part_, g).start()

    def y_in(part_, g):
        piece = (part_,) + mine

        @pl.when(y != 0)
        def _():
            links.copy(wr.at[piece], wr.at[piece], ysc + g, "y", 0).wait_recv()

        return gather_stage(links, "y", wr, piece)

    def x_out(g):
        @pl.when(origin)
        def _():
            @pl.when(k == 1)
            def _():
                core_copies[g].wait_recv()
            for j in range(1, NX):
                xscatter(j, g).start()
            stgx[g] = stgk[g, :, 0:512]

    def z_out(g):
        @pl.when(z == 0)
        def _():
            @pl.when(x != 0)
            def _():
                links.copy(stgx.at[g], stgx.at[g], xsc + g, "x", 0).wait_recv()
            for j in range(1, NZ):
                zscatter(j, g).start()
            wc[(g,) + zregion(links)] = stgx[(g,) + zpiece(0)]

    def z_in(g):
        region = (g,) + zregion(links)

        @pl.when(z != 0)
        def _():
            links.copy(wc.at[region], wc.at[region], zsc + g, "z", 0).wait_recv()

        return gather_stage(links, "z", wc, region)

    def direct(j):
        return links.copy(wsrc.at[lo], wr.at[lo], ysc, "y", j)

    @pl.when(y == 0)
    def _():
        for j in (4, 3, 5, 2, 6, 1, 7):
            direct(j).start()
        wr[0] = wsrc[0]

    @pl.when(row == 0)
    def _():
        core_copies[0].start()
        stgk[0] = a_ref[0:48, :]
        for copy in core_copies[1:]:
            copy.start()

    x_out(0)

    @pl.when(row == 0)
    def _():
        stgk[1] = a_ref[96:144, :]
        stgk[2] = a_ref[192:240, :]

    @pl.when(row == 1)
    def _():
        stgk[2, 16:48, :] = a_ref[0:32, :]

    z_out(0)

    gl_r = row * ROWS + lax.broadcasted_iota(jnp.int32, (B, ROWS), 1)
    gl_c = y * COLS + lax.broadcasted_iota(jnp.int32, (B, COLS), 1)
    lane128 = lax.broadcasted_iota(jnp.int32, (B, 128), 1)
    first_col = y == 0

    def chunks(step):
        def run(i, _):
            step(pl.ds(pl.multiple_of(512 * i, 512), 512))
            return 0
        lax.fori_loop(0, 4, run, 0)

    def product_cols(pr, mat, out):
        def step(lanes):
            out[:, lanes] = nn(pr, mat[:, lanes])
        chunks(step)

    def product_rows(pc, mat, width):
        def step(i, acc):
            lanes = pl.ds(pl.multiple_of(512 * i, 512), 512)
            return acc + nt(pc[:, lanes], mat[:, lanes])
        return lax.fori_loop(0, 4, step, jnp.zeros((B, width), F32))

    def widen(m):
        sq[...] = jnp.zeros((B, 128), F32)
        sq[:, 0:B] = m
        return sq[...]

    def square(window, at):
        width = window.shape[1]
        return jnp.where(lane128 < B, pltpu.roll(window, width - at, axis=1)[:, 0:128], 0.0)

    def col_square(ref, at):
        return jnp.where(first_col, square(ref[:, 0:384], at), 0.0)

    def scale_of(gram):
        eye = lax.broadcasted_iota(jnp.int32, (B, 128), 0) == lane128
        diagonal = jnp.sum(jnp.where(eye, gram, 0.0), axis=1, keepdims=True)
        return lax.rsqrt(jnp.max(diagonal, axis=0, keepdims=True))

    def unit_part(chol, trail):
        wide = jnp.concatenate([widen(chol), jnp.zeros((B, 384), F32)], axis=1)
        return pltpu.roll(wide, trail, axis=1)

    def make_k(unit, p):
        kc[...] = -pcs[p]
        kc[:, 0:512] = kc[:, 0:512] + jnp.where(first_col, unit, 0.0)
        return (jnp.where(row == 0, unit[:, 0:256], 0.0) + jnp.where(row == 1, unit[:, 256:512], 0.0)) - prs[p]

    @pl.when(y != 0)
    def _():
        links.copy(wr.at[lo], wr.at[lo], ysc, "y", 0).wait_recv()

    prs[0] = jnp.where(gl_r >= B, wr[0], 0.0)
    product_cols(prs[0], a_ref, part.at[0])
    ps = psum_core(links, part.at[0], bufk.at[0])

    @pl.when(y == 0)
    def _():
        t = a_ref[:, 0:384].T
        wsrc[1] = t[B:2 * B]
        wsrc[2] = t[2 * B:3 * B]

    y_out(hi, 1)
    w0 = z_in(0)
    ps = psum_x(links, ps, part.at[0], bufk.at[0], sumk.at[0], bufx.at[0])
    arrive(w0)
    w0 = gather_stage(links, "x", wc, (0,) + xregion(links))
    ps = psum_z(links, ps, sumk.at[0], bufx.at[0], sumx.at[0], bufz.at[0])
    x_out(1)
    wr_hi = y_in(hi, 1)
    arrive(w0)
    w0 = gather_stage(links, "k", wc, (0,) + kregion(links))
    ps = psum_back_z(links, ps, sumx.at[0], bufz.at[0], yc.at[0])
    z_out(1)
    arrive(w0)
    pcs[0] = jnp.where(gl_c >= B, wc[0], 0.0)
    gsrc[0, 0, :, 0:128] = widen(product_rows(pcs.at[0], pcs.at[0], B))
    gsrc[0, 0, :, 128:256] = col_square(pcs.at[0], B)
    gs = half_start(links, gsrc.at[0, 0], gparts, ghead, hsem + 1)
    rsrc[0, 0] = product_rows(pcs.at[0], a_ref, ROWS)
    arrive(ps)
    ps = gather_stage(links, "x", yc.at[0], xregion(links))
    w1 = z_in(1)
    gs = half_mid(links, gs, gparts, ghead, hsem + 1, gres.at[0, 0])
    rs = ysum_start(links, rsrc.at[0], rbuf.at[0])
    x_out(2)
    arrive(ps)
    ps = gather_stage(links, "k", yc.at[0], kregion(links))
    arrive(w1)
    w1 = gather_stage(links, "x", wc, (1,) + xregion(links))
    arrive(ps)
    arrive(gs)
    scale = scale_of(gres[0, 0, :, 0:128])
    pcs[0] = pcs[0] * scale
    prs[0] = prs[0] * scale
    im[...] = yc[0] * scale
    csrc[:, 0:128] = widen(product_rows(pcs.at[0], im, B))
    csrc[:, 128:256] = col_square(im, B)
    cs = half_start(links, csrc, cparts, chead, hsem)
    rs = ysum_mid(links, rs, rsrc.at[0], rbuf.at[0], rres.at[0])
    z_out(2)
    top = gres[0, 0, :, 128:256] * scale
    state = factor_some(0, 6, factor_start(gres[0, 0, :, 0:128] * scale * scale, top))
    arrive(w1)
    w1 = gather_stage(links, "k", wc, (1,) + kregion(links))
    state = factor_some(6, 8, state)
    arrive(w1)
    esrc[0, :, 0:128] = col_square(wc.at[1], B)
    esrc[0, :, 128:256] = col_square(im, 2 * B)
    esrc[1, :, 0:128] = col_square(pcs.at[0], 2 * B)
    esrc[1, :, 128:256] = col_square(wc.at[1], 2 * B)
    es = ysum_start(links, esrc, ebuf)
    cs = half_mid(links, cs, cparts, chead, hsem, cres)
    state = factor_some(8, 12, state)
    low, nt_, inv = factor_end(state)
    unit = unit_part(low, B)
    kr = make_k(unit, 0)

    def image(lanes):
        yy[:, lanes] = nn(low, wc[1, :, lanes]) - im[:, lanes]
    chunks(image)
    es = ysum_mid(links, es, esrc, ebuf, eres)
    w2 = z_in(2)
    arrive(rs)
    arrive(wr_hi)
    yrow = rres[0, 0] * scale
    yr = nn(low, wr[1]) - yrow
    arrive(cs)

    yt, phi = cres[:, 128:128 + B], cres[:, 0:B]
    of_k = -nn(inv, nt(nt(yt, low) - phi, nt_))
    of_both = jnp.concatenate([inv, of_k], axis=1)

    def next_panel(lanes):
        pcs[1, :, lanes] = nn(of_both, jnp.concatenate([im[:, lanes], kc[:, lanes]], axis=0))
    chunks(next_panel)
    pcs[1] = jnp.where(gl_c >= 2 * B, pcs[1], 0.0)
    gsrc[1, 0, :, 0:128] = widen(product_rows(pcs.at[1], pcs.at[1], B))
    gsrc[1, 0, :, 128:256] = col_square(pcs.at[1], 2 * B)
    gs = ysum_start(links, gsrc.at[1], gbuf.at[1])
    prs[1] = jnp.where(gl_r >= 2 * B, nn(of_both, jnp.concatenate([yrow, kr], axis=0)), 0.0)
    arrive(w2)
    w2 = gather_stage(links, "x", wc, (2,) + xregion(links))

    def coupling(low, nt_, att, yt, phi):
        c = nt(nn(low, att) - yt, low) - nt(low, yt) + phi
        return -0.5 * nt(nn(nt_, c), nt_)

    arrive(es)
    nd = coupling(low, nt_, eres[0, :, 0:B], yt, phi)
    hr = nn(nt_, yr) + nn(nd, kr)
    right_r = jnp.concatenate([kr, hr], axis=0)
    left = jnp.concatenate([hr, kr], axis=0).T
    of_h = jnp.concatenate([nt_, nd], axis=1)

    prow = prs[1]

    def update(i, acc):
        lanes = pl.ds(pl.multiple_of(512 * i, 512), 512)
        kcl = kc[:, lanes]
        hcl = nn(of_h, jnp.concatenate([yy[:, lanes], kcl], axis=0))
        hc[:, lanes] = hcl
        fresh = a_ref[:, lanes] - nn(left, jnp.concatenate([kcl, hcl], axis=0))
        o_ref[:, lanes] = fresh
        part[1, :, lanes] = nn(prow, fresh)
        return acc + nt(pcs[1, :, lanes], fresh)
    rsrc[1, 0] = lax.fori_loop(0, 4, update, jnp.zeros((B, ROWS), F32))
    rs = ysum_start(links, rsrc.at[1], rbuf.at[1])
    ps = psum_core(links, part.at[1], bufk.at[1])
    gs = ysum_mid(links, gs, gsrc.at[1], gbuf.at[1], gres.at[1])
    arrive(w2)
    w2 = gather_stage(links, "k", wc, (2,) + kregion(links))
    ps = psum_x(links, ps, part.at[1], bufk.at[1], sumk.at[1], bufx.at[1])
    kt = -eres[1, :, 0:B]
    ht = nn(nt_, nn(low, eres[1, :, 128:128 + B]) - eres[0, :, 128:128 + B]) + nn(nd, kt)
    rows2 = jnp.concatenate([ht, kt], axis=0).T
    aer[...] = wr[2] - nn(rows2, right_r)
    arrive(w2)
    fsrc[0, :, 0:128] = col_square(wc.at[2], 2 * B)
    fsrc[0, :, 128:256] = jnp.zeros((B, 128), F32)
    fs = ysum_start(links, fsrc, fbuf)

    def next_rows(lanes):
        aec[:, lanes] = wc[2, :, lanes] - nn(rows2, jnp.concatenate([kc[:, lanes], hc[:, lanes]], axis=0))
    chunks(next_rows)
    rs = ysum_mid(links, rs, rsrc.at[1], rbuf.at[1], rres.at[1])
    ps = psum_z(links, ps, sumk.at[1], bufx.at[1], sumx.at[1], bufz.at[1])
    arrive(gs)
    scale = scale_of(gres[1, 0, :, 0:128])
    pcs[1] = pcs[1] * scale
    prs[1] = prs[1] * scale
    top = gres[1, 0, :, 128:256] * scale
    state = factor_some(0, 5, factor_start(gres[1, 0, :, 0:128] * scale * scale, top))
    arrive(rs)
    yrow = rres[1, 0] * scale
    none = jnp.zeros((B, ROWS), F32)
    ssrc[:, 0:128] = widen(nt(prs[1], yrow))
    ssrc[:, 128:256] = (jnp.where(row == 0, square(jnp.concatenate([yrow, none], axis=1), 2 * B), 0.0)
                        + jnp.where(row == 1, square(jnp.concatenate([none, yrow], axis=1), 2 * B), 0.0))
    ss = small_core(links, ssrc, sk)
    fs = ysum_mid(links, fs, fsrc, fbuf, fres)
    ps = psum_back_z(links, ps, sumx.at[1], bufz.at[1], yc.at[1])
    ss = small_next(links, ss, "x", sk, sx)
    state = factor_some(5, 9, state)
    ss = small_next(links, ss, "z", sx, sz)
    arrive(ps)
    ps = gather_stage(links, "x", yc.at[1], xregion(links))
    state = factor_some(9, 12, state)
    kt1, ht1 = kt, ht
    low, nt_, _ = factor_end(state)
    ss = small_back(links, ss, sz, sres)
    arrive(ps)
    ps = gather_stage(links, "k", yc.at[1], kregion(links))
    kr = make_k(unit_part(low, 2 * B), 1)
    yr = nn(low, aer[...]) - yrow
    nty = nn(nt_, yr)

    def image_free(lanes):
        yy[:, lanes] = nn(low, aec[:, lanes])
    chunks(image_free)
    arrive(fs)
    att = fres[0, :, 0:B] - nn(rows2, jnp.concatenate([kt1, ht1], axis=0))
    arrive(ps)
    arrive(ss)
    nd = coupling(low, nt_, att, sres[:, 128:128 + B], sres[:, 0:B])
    left = jnp.concatenate([nty + nn(nd, kr), kr], axis=0).T
    of_h = jnp.concatenate([nt_, nd], axis=1)

    def last(lanes):
        kcl = kc[:, lanes]
        hcl = nn(of_h, jnp.concatenate([yy[:, lanes] - yc[1, :, lanes] * scale, kcl], axis=0))
        o_ref[:, lanes] = o_ref[:, lanes] - nn(left, jnp.concatenate([kcl, hcl], axis=0))
    chunks(last)

    @pl.when(y == 0)
    def _():
        links.take(send.at[ysc], (NY - 1) * B * ROWS)
        links.take(send.at[ysc + 1], (NY - 1) * 2 * 24 * 128)
        links.take(send.at[hsem], (NY - 1) * 48 * 128)
        links.take(send.at[hsem + 1], (NY - 1) * 48 * 128)

    @pl.when(row == 0)
    def _():
        for copy in core_copies:
            copy.wait_send()

    @pl.when(origin)
    def _():
        for g in range(3):
            links.take(send.at[xsc + g], (NX - 1) * 48 * 512)

    @pl.when(z == 0)
    def _():
        for g in range(3):
            links.take(send.at[zsc + g], (NZ - 1) * 24 * 128)

    links.finish()


def local(matrix):
    vmem = pltpu.VMEM

    def ysum_buffers(lead, n):
        return [vmem(lead + (n, B, 256), F32), vmem(lead + (NY, n, 24, 128), F32), vmem(lead + (n, B, 256), F32)]

    return pl.pallas_call(
        body,
        out_shape=jax.ShapeDtypeStruct((ROWS, COLS), F32),
        in_specs=[pl.BlockSpec(memory_space=pltpu.VMEM)],
        out_specs=pl.BlockSpec(memory_space=pltpu.VMEM),
        scratch_shapes=[
            vmem((3, B, ROWS), F32), vmem((3, B, ROWS), F32), vmem((3, B, COLS), F32),
            vmem((3, 48, COLS), F32), vmem((3, 48, 512), F32),
            vmem((2, B, COLS), F32), vmem((2, 48, COLS), F32), vmem((2, 48, COLS), F32),
            vmem((2, NX, 48, 512), F32), vmem((2, 48, 512), F32), vmem((2, NZ, 24, 128), F32), vmem((2, B, COLS), F32),
            *ysum_buffers((2,), 1), *ysum_buffers((2,), 1), vmem((B, 256), F32), vmem((NY, 48, 128), F32), vmem((48, 128), F32), vmem((B, 256), F32),
            vmem((NY, 48, 128), F32), vmem((48, 128), F32), *ysum_buffers((), 2), *ysum_buffers((), 1),
            vmem((B, 256), F32), vmem((2, 24, 128), F32), vmem((NX, 24, 128), F32), vmem((NZ, 24, 128), F32), vmem((B, 256), F32),
            vmem((2, B, COLS), F32), vmem((2, B, ROWS), F32), vmem((B, COLS), F32), vmem((B, ROWS), F32),
            vmem((B, COLS), F32), vmem((B, COLS), F32), vmem((B, COLS), F32), vmem((B, COLS), F32), vmem((B, 128), F32),
            vmem((METER, 128), F32),
            pltpu.SemaphoreType.DMA((SEMS,)), pltpu.SemaphoreType.DMA((SEMS,)),
        ],
        compiler_params=pltpu.CompilerParams(
            collective_id=0, has_side_effects=True, vmem_limit_bytes=56 * 1024 * 1024),
        name="two_panels",
    )(matrix)


def solution(mesh):
    return jax.shard_map(local, mesh=mesh, in_specs=(P("row", "col"),), out_specs=P("row", "col"), check_vma=False)
```
